768 devices in a mesh: batch: 128 (over y, x, z_hi, core), tower: 6 (over z_lo).
Axes of the slice: x: 4, y: 8, z: 12 (z_hi: 2, z_lo: 6; z = z_hi * 6 + z_lo), core: 2. Of those that a mesh axis runs over, the one named last changes fastest.
Arguments:
- image_features: bfloat16 [18432, 1152], P('batch', 'tower'), may hold values from -6 to 6
- text_features: bfloat16 [18432, 1152], P('batch', 'tower'), may hold values from -6 to 6
- image_head: bfloat16 [1152, 1152], P('tower'), may hold values from -0.1875 to 0.1875
- text_head: bfloat16 [1152, 1152], P('tower'), may hold values from -0.1875 to 0.1875
- caption_ids: int32 [18432], replicated, may hold values from 0 to 9215
- logit_scale: float32 [1], replicated, may hold values from 5 to 20
- logit_bias: float32 [1], replicated, may hold values from -4 to -1
Outputs:
- loss: float32 [1], replicated
- image_head_grad: float32 [1152, 1152], P('tower')
- text_head_grad: float32 [1152, 1152], P('tower')
The draws below stay inside these ranges and needn't reach their ends.
Inputs may be any that keep to these rules, and one draw needn't show every extreme that they name: `caption_ids`: image and caption of slots with equal ids count as matching pairs.
All inputs are finite; a program needn't handle non-finite values.
Results may differ from the reference program's by a relative error of at most 0.0033.
Values may be sent and summed in bfloat16 or wider, within the bound.
A program may use at most 64 MiB of HBM per device.

```python
import math
import jax
import jax.numpy as jnp
from jax import lax

E = 1152
DW = 1152
ROWS = 144
BATCH = 18432
N_BATCH = 128


def touch_ends(drawn, key, least, high):
    spot = [jax.random.randint(jax.random.fold_in(key, axis), (), 0, length) for axis, length in enumerate(drawn.shape)]
    main_axis = drawn.shape.index(max(drawn.shape))
    neighbour = spot[:main_axis] + [(spot[main_axis] + 1) % drawn.shape[main_axis]] + spot[main_axis + 1:]
    return drawn.at[tuple(spot)].set(least).at[tuple(neighbour)].set(high)


def level_of(stream_key, shape, cuts, low, largest):
    gain = 1.0
    for dim, shards_of in cuts:
        draws = jax.random.uniform(jax.random.fold_in(jax.random.fold_in(stream_key, 6), dim), (shards_of,), jnp.float32, low / len(cuts), largest / len(cuts))
        gain = gain * jnp.repeat(jnp.exp(draws), shape[dim] // shards_of).reshape((-1,) + (1,) * (len(shape) - 1 - dim))
    return gain


def centred(stream_key, shape, width, reach, cuts=(), held_as=jnp.bfloat16):
    entries = width * jax.random.normal(stream_key, shape, jnp.float32)
    if cuts:
        entries = entries * level_of(stream_key, shape, cuts, -0.22, 0.18)
    return jnp.clip(entries, -reach, reach).astype(held_as)


def setup_inputs(seed: int = 0) -> dict:
    key_of = jax.random.split(jax.random.key(seed), 8)
    image_features = centred(key_of[0], (BATCH, DW), 1.0, 6.0, ((0, 128), (1, 6)))
    text_features = centred(key_of[1], (BATCH, DW), 1.0, 6.0, ((0, 128), (1, 6)))
    image_head = centred(key_of[2], (DW, E), DW ** -0.5, 0.1875, ((0, 6),))
    text_head = centred(key_of[3], (DW, E), DW ** -0.5, 0.1875, ((0, 6),))
    caption_ids = touch_ends(jax.random.randint(key_of[4], (BATCH,), 0, BATCH // 2), jax.random.fold_in(key_of[4], 1), 0, (BATCH // 2) - 1).astype(jnp.int32)
    logit_scale = jnp.clip(jnp.exp(jax.random.uniform(key_of[5], (1,), jnp.float32, math.log(5.0), math.log(20.0))), 5.0, 20.0)
    logit_bias = jnp.clip(jax.random.uniform(key_of[6], (1,), jnp.float32, -4.0, -1.0), -4.0, -1.0)
    return dict(image_features=image_features, text_features=text_features, image_head=image_head, text_head=text_head, caption_ids=caption_ids, logit_scale=logit_scale, logit_bias=logit_bias)


norm_eps = 1e-06

def normalize(unscaled):
    inverse = lax.rsqrt(lax.optimization_barrier(jnp.sum(unscaled * unscaled, axis=-1, keepdims=True)) + norm_eps)
    return (unscaled * inverse, inverse)

def backward_norm(grad, unit, inverse):
    return (inverse * (grad - unit * lax.optimization_barrier(jnp.sum(unit * grad, axis=-1, keepdims=True)))).astype(jnp.bfloat16)

def reference(image_features, text_features, image_head, text_head, caption_ids, logit_scale, logit_bias):
    image_raw = jnp.dot(image_features, image_head, preferred_element_type=jnp.float32)
    text_raw = jnp.dot(text_features, text_head, preferred_element_type=jnp.float32)
    image_unit, image_inverse = normalize(image_raw)
    text_unit, text_inverse = normalize(text_raw)
    image_embed = image_unit.astype(jnp.bfloat16)
    text_embed = text_unit.astype(jnp.bfloat16)
    logit_mult = logit_scale[0]
    logit_shift = logit_bias[0]
    image_blocks = image_embed.reshape(N_BATCH, ROWS, E)
    id_blocks = caption_ids.reshape(N_BATCH, ROWS)

    def one_block(running, inputs):
        text_acc, loss_acc = running
        block_embed, block_ids = inputs
        logits = logit_mult * jnp.dot(block_embed, text_embed.T, preferred_element_type=jnp.float32) + logit_shift
        sign_table = jnp.where(block_ids[:, None] == caption_ids[None, :], 1.0, -1.0).astype(jnp.float32)
        loss_acc = loss_acc - jnp.sum(jax.nn.log_sigmoid(sign_table * logits)) / BATCH
        pair_coef = (-(sign_table * logit_mult / BATCH) * jax.nn.sigmoid(-sign_table * logits)).astype(jnp.bfloat16)
        image_part = jnp.dot(pair_coef, text_embed, preferred_element_type=jnp.float32)
        text_acc = text_acc + jnp.dot(pair_coef.T, block_embed, preferred_element_type=jnp.float32)
        return ((text_acc, loss_acc), image_part)
    start_state = (jnp.zeros((BATCH, E), jnp.float32), jnp.zeros((), jnp.float32))
    (text_grad, loss_value), image_parts = lax.scan(one_block, start_state, (image_blocks, id_blocks))
    image_grad = image_parts.reshape(BATCH, E)
    image_delta = backward_norm(image_grad, image_unit, image_inverse)
    text_delta = backward_norm(text_grad, text_unit, text_inverse)
    image_head_grad = jnp.dot(image_features.T, image_delta, preferred_element_type=jnp.float32)
    text_head_grad = jnp.dot(text_features.T, text_delta, preferred_element_type=jnp.float32)
    return (loss_value.reshape(1), image_head_grad, text_head_grad)
```

```python
import functools

import jax
import jax.numpy as jnp
from jax import lax
from jax.experimental import pallas as pl
from jax.experimental.pallas import tpu as pltpu
from jax.sharding import PartitionSpec as P

MESH = pl.DeviceIdType.MESH
F32, BF16 = jnp.float32, jnp.bfloat16
NX, NY, NZ, NT = 4, 8, 12, 6
E = 1152
U = 48
NI, NJ = NZ * U, 4 * NX * U
norm_eps = 1e-06


def place():
    b = lax.axis_index("batch")
    zl = lax.axis_index("tower")
    c = lax.rem(b, 2)
    zh = lax.rem(b // 2, 2)
    x = lax.rem(b // 4, NX)
    y = b // 16
    return x, y, zh, zl, c


def device(x, y, z, c):
    return (((y * NX + x) * 2 + z // NT) * 2 + c, lax.rem(z, NT))


def rows(i, n=U):
    return pl.ds(pl.multiple_of(i * n, 8 if n % 16 else 16), n)


def copy(src, dst, ss, rs, dev):
    return pltpu.make_async_remote_copy(
        src_ref=src, dst_ref=dst, send_sem=ss, recv_sem=rs, device_id=dev, device_id_type=MESH
    )


def kernel(
    fi, ft, hi, ht, ids_i, ids_t, scale, bias,
    out, loss_out,
    h, fx, fa, part, spart, rpart, unit, inv,
    img, txt, own, ip, coef, gi, gt, gix, zs, zr, gtb, xr, ys, yr, gsum, gland,
    delta, g, ax, a, ap, ay, az, ag, lp, lc, lt, lx,
    hsem, fs, fr, ps, pr, isn, irc, ic_s, ic_r, ts_s, ts_r, ys_s, ys_r, xs_s, xs_r,
    gx_s, gx_r, zs_s, zs_r, xr_s, xr_r, yr_s, yr_r, gl_s, gl_r, d_s, d_r,
    ax_s, ax_r, ay_s, ay_r, az_s, az_r, ag_s, ag_r, o_s, o_r, oc_s, oc_r,
    lc_s, lc_r, lt_s, lt_r, lx_s, lx_r,
):
    x, y, zh, zl, c = place()
    z = zh * NT + zl
    other = device(x, y, z, 1 - c)
    half = y // 4

    def at_x(k):
        xx = lax.rem(x + k, NX)
        return xx, device(xx, y, z, c)

    def at_y(yy):
        return device(x, yy, z, c)

    def at_z(zz):
        return device(x, y, zz, c)

    @pl.when(c == 0)
    def _():
        pltpu.make_async_copy(hi, h, hsem).start()

    @pl.when(c == 1)
    def _():
        pltpu.make_async_copy(ht, h, hsem).start()

    barrier = pltpu.get_barrier_semaphore()

    def greet(dev):
        pl.semaphore_signal(barrier, inc=1, device_id=dev, device_id_type=MESH)

    greet(other)
    for k in range(1, NX):
        greet(at_x(k)[1])
    for k in range(1, NY):
        greet(at_y(lax.rem(y + k, NY)))
    for k in range(1, NZ):
        greet(at_z(lax.rem(z + k, NZ)))
    pl.semaphore_wait(barrier, 1 + NX - 1 + NY - 1 + NZ - 1)

    @pl.when(c == 0)
    def _():
        copy(ft, fx, fs, fr, other).start()

    @pl.when(c == 1)
    def _():
        copy(fi, fx, fs, fr, other).start()

    copy(ft, fx, fs, fr, other).wait()

    def gather_features(first, second):
        fst = first[...].astype(F32)
        snd = second[...].astype(F32)
        for t in range(NT):
            fa[t * U : (t + 1) * U, :] = jnp.concatenate(
                [fst[24 * t : 24 * t + 24], snd[24 * t : 24 * t + 24]], axis=0
            ).astype(BF16)

    @pl.when(c == 0)
    def _():
        gather_features(fi, fx)

    @pl.when(c == 1)
    def _():
        gather_features(fx, ft)

    pltpu.make_async_copy(hi, h, hsem).wait()

    part[...] = jnp.dot(fa[...], h[...], preferred_element_type=F32)
    spart[...] = part[...].astype(BF16)

    def part_copy(to):
        return copy(
            spart.at[rows(to)], rpart.at[rows(zl)], ps.at[to], pr.at[zl], at_z(zh * NT + to)
        )

    def part_wait(src):
        copy(spart.at[rows(0)], rpart.at[rows(src)], ps.at[0], pr.at[src], other).wait_recv()

    for k in range(1, NT):
        part_copy(lax.rem(zl + k, NT)).start()
    raw = part[rows(zl), :]
    for k in range(1, NT):
        src = lax.rem(zl + k, NT)
        part_wait(src)
        raw = raw + rpart[rows(src), :].astype(F32)
    inverse = lax.rsqrt(jnp.sum(raw * raw, axis=-1, keepdims=True) + norm_eps)
    raw = raw * inverse
    unit[...] = raw
    inv[...] = jnp.broadcast_to(inverse, (U, 128))
    own[...] = raw.astype(BF16)

    mine = rows(lax.rem(y, 4) * NX + x)

    def img_up(slot):
        return copy(
            img.at[rows(slot)], img.at[rows(slot)], isn.at[0, slot], irc.at[slot],
            at_z(lax.rem(z + 1, NZ)),
        )

    def img_down(slot):
        return copy(
            img.at[rows(slot)], img.at[rows(slot)], isn.at[1, slot], irc.at[slot],
            at_z(lax.rem(z + NZ - 1, NZ)),
        )

    def img_over(slot):
        return copy(
            img.at[rows(slot)], img.at[rows(slot)], ic_s.at[slot], ic_r.at[slot], other
        )

    def txt_over():
        return copy(own, txt.at[mine], ts_s, ts_r, other)

    def txt_y(to):
        return copy(txt.at[mine], txt.at[mine], ys_s.at[to], ys_r.at[lax.rem(y, 4)], at_y(to))

    def txt_x(yi, k):
        xx, dev = at_x(k)
        slot = rows(yi * NX + x)
        return copy(txt.at[slot], txt.at[slot], xs_s.at[yi, xx], xs_r.at[yi, x], dev)

    def txt_y_send():
        for k in (4, 3, 5, 2, 6, 1, 7):
            txt_y(lax.rem(y + k, NY)).start()

    def txt_forward(k):
        yi = lax.rem(y + k, 4)

        @pl.when(4 * c + yi != y)
        def _():
            slot = rows(yi * NX + x)
            copy(txt.at[slot], txt.at[slot], ys_s.at[0], ys_r.at[yi], other).wait_recv()

        for kx in (2, 1, 3):
            txt_x(yi, kx).start()

    @pl.when(c == 1)
    def _():
        @pl.when(half == 0)
        def _():
            txt_over().start()

        @pl.when(half == 1)
        def _():
            txt[mine, :] = own[...]
            txt_y_send()

        for k in range(4):
            txt_forward(k)
        for s in range(NZ):
            img_over(s).wait_recv()

    @pl.when(c == 0)
    def _():
        img[rows(z), :] = own[...]
        img_up(z).start()
        img_down(z).start()
        img_over(z).start()

        @pl.when(half == 0)
        def _():
            txt_over().wait_recv()
            txt_y_send()

        for s in range(1, 7):
            lo = lax.rem(z + NZ - s, NZ)
            hi_ = lax.rem(z + s, NZ)
            img_up(lo).wait_recv()
            if s < 6:
                img_up(lo).start()
            img_over(lo).start()
            if s < 6:
                img_down(hi_).wait_recv()
                if s < 5:
                    img_down(hi_).start()
                img_over(hi_).start()
            if s <= 4:
                txt_forward(s - 1)

    for yi in range(4):
        for k in range(1, NX):
            xx = lax.rem(x + k, NX)
            slot = rows(yi * NX + xx)
            copy(txt.at[slot], txt.at[slot], xs_s.at[0, 0], xs_r.at[yi, xx], other).wait_recv()

    ip[...] = lax.dot_general(
        img[...], txt[...], (((1,), (1,)), ((), ())), preferred_element_type=F32
    )
    mult, shift = scale[0], bias[0]
    factor = mult * (1.0 / (NX * NY * NZ * U))

    def pairs(i, total):
        r = rows(i)
        logits = mult * ip[r, :] + shift
        same = ids_i[r, :] == ids_t[...]
        v = jnp.where(same, logits, -logits)
        e = jnp.exp(-jnp.abs(v))
        d = 1.0 / (1.0 + e)
        sig = jnp.where(v >= 0, e * d, d)
        coef[r, :] = (jnp.where(same, -factor, factor) * sig).astype(BF16)
        ls = jnp.log1p(e) - jnp.minimum(v, 0.0)
        ls = jnp.sum(ls.reshape(U // 8, 8, NJ), axis=0)
        for j in range(NJ // 128):
            total = total + ls[:, 128 * j : 128 * (j + 1)]
        return total

    lp[...] = lax.fori_loop(0, NZ, pairs, jnp.zeros((8, 128), F32))

    def lc_copy():
        return copy(lp, lc, lc_s, lc_r, other)

    lc_copy().start()

    def gx_copy(q, to_core):
        return copy(gi.at[rows(2 * q + to_core)], gix.at[rows(q)], gx_s.at[q], gx_r.at[q], other)

    gi[...] = jnp.dot(coef[...], txt[...], preferred_element_type=F32)
    for q in range(NZ // 2):
        gx_copy(q, 1 - c).start()

    gt[...] = lax.dot_general(
        coef[...], img[...], (((0,), (0,)), ((), ())), preferred_element_type=F32
    )

    def xr_copy(yi, k):
        xx, dev = at_x(k)
        return copy(
            gtb.at[rows(yi * NX + xx)], xr.at[rows(yi * NX + x)], xr_s.at[yi, xx], xr_r.at[yi, x],
            dev,
        )

    for k in range(4):
        yi = lax.rem(y + 1 + k, 4)
        blk = rows(yi, NX * U)
        gtb[blk, :] = gt[blk, :].astype(BF16)
        for kx in (2, 1, 3):
            xr_copy(yi, kx).start()

    def zs_copy(q):
        to = 2 * q + c
        return copy(zs.at[rows(q)], zr.at[rows(z)], zs_s.at[q], zr_r.at[z], at_z(to))

    zr_r = zs_r
    for k in range(NZ // 2):
        q = lax.rem(z // 2 + 3 + k, 6)
        gx_copy(q, c).wait_recv()
        to = 2 * q + c
        s = gi[rows(to), :] + gix[rows(q), :]
        zs[rows(q), :] = s.astype(BF16)

        @pl.when(to != z)
        def _():
            zs_copy(q).start()

        @pl.when(to == z)
        def _():
            gsum[0] = s

    def yr_copy(yi):
        to = 4 * c + yi
        return copy(ys.at[rows(yi)], yr.at[rows(y)], yr_s.at[yi], yr_r.at[y], at_y(to))

    for k in range(4):
        yi = lax.rem(y + 1 + k, 4)
        s = gt[rows(yi * NX + x), :]
        for kx in range(1, NX):
            xx = lax.rem(x + kx, NX)
            slot = rows(yi * NX + xx)
            copy(gtb.at[slot], xr.at[slot], xr_s.at[0, 0], xr_r.at[yi, xx], other).wait_recv()
            s = s + xr[slot, :].astype(F32)
        ys[rows(yi), :] = s.astype(BF16)

        @pl.when(4 * c + yi != y)
        def _():
            yr_copy(yi).start()

        @pl.when(4 * c + yi == y)
        def _():
            gsum[1] = s

    def gl_copy(m):
        return copy(gsum.at[m], gland, gl_s, gl_r, other)

    @pl.when(lax.rem(z, 2) == c)
    def _():
        s = gsum[0]
        for k in range(1, NZ):
            src = lax.rem(z + k, NZ)
            copy(zs.at[rows(0)], zr.at[rows(src)], zs_s.at[0], zr_r.at[src], other).wait_recv()
            s = s + zr[rows(src), :].astype(F32)
        gsum[0] = s

        @pl.when(c == 1)
        def _():
            gl_copy(0).start()

    @pl.when(half == c)
    def _():
        s = gsum[1]
        for k in range(1, NY):
            src = lax.rem(y + k, NY)
            copy(ys.at[rows(0)], yr.at[rows(src)], yr_s.at[0], yr_r.at[src], other).wait_recv()
            s = s + yr[rows(src), :].astype(F32)
        gsum[1] = s

        @pl.when(c == 0)
        def _():
            gl_copy(1).start()

    @pl.when(jnp.logical_and(c == 0, lax.rem(z, 2) == 1))
    def _():
        gl_copy(0).wait_recv()
        gsum[0] = gland[...]

    @pl.when(jnp.logical_and(c == 1, half == 0))
    def _():
        gl_copy(0).wait_recv()
        gsum[1] = gland[...]

    grad = gsum[c]
    un = unit[...]
    dl = inv[:, 0:1] * (grad - un * jnp.sum(un * grad, axis=-1, keepdims=True))
    delta[rows(zl), :] = dl.astype(BF16)

    lc_copy().wait_recv()
    lt[rows(zl, 8), :] = lp[...] + lc[...]

    def d_copy(to):
        return copy(
            delta.at[rows(zl)], delta.at[rows(zl)], d_s.at[to], d_r.at[zl], at_z(zh * NT + to)
        )

    def lt_copy(to):
        return copy(
            lt.at[rows(zl, 8)], lt.at[rows(zl, 8)], lt_s.at[to], lt_r.at[zl], at_z(zh * NT + to)
        )

    for k in range(1, NT):
        to = lax.rem(zl + k, NT)
        d_copy(to).start()
        lt_copy(to).start()
    for k in range(1, NT):
        src = lax.rem(zl + k, NT)
        copy(delta.at[rows(0)], delta.at[rows(src)], d_s.at[0], d_r.at[src], other).wait_recv()
        copy(lt.at[rows(0, 8)], lt.at[rows(src, 8)], lt_s.at[0], lt_r.at[src], other).wait_recv()
    ls = lt[0:8, :]
    for t in range(1, NT):
        ls = ls + lt[8 * t : 8 * t + 8, :]
    lx[rows(x, 8), :] = ls

    g[...] = lax.dot_general(
        fa[...], delta[...], (((0,), (0,)), ((), ())), preferred_element_type=F32
    )

    def ax_copy(k):
        xx, dev = at_x(k)
        return copy(g.at[rows(xx)], ax.at[rows(x)], ax_s.at[xx], ax_r.at[x], dev)

    def lx_copy(k):
        xx, dev = at_x(k)
        return copy(lx.at[rows(x, 8)], lx.at[rows(x, 8)], lx_s.at[xx], lx_r.at[x], dev)

    for k in (2, 1, 3):
        ax_copy(k).start()
        lx_copy(k).start()
    s = g[rows(x), :]
    for k in range(1, NX):
        xx = lax.rem(x + k, NX)
        copy(g.at[rows(0)], ax.at[rows(xx)], ax_s.at[0], ax_r.at[xx], other).wait_recv()
        s = s + ax[rows(xx), :]
        copy(lx.at[rows(0, 8)], lx.at[rows(xx, 8)], lx_s.at[0], lx_r.at[xx], other).wait_recv()
    for k in range(NY):
        ap[k, 0:U, :] = s[:, 128 * k : 128 * (k + 1)]
    for k in range(6):
        ap[k, U : U + 8, :] = s[8 * k : 8 * k + 8, 1024:1152]
    ls = lx[0:8, :]
    for t in range(1, NX):
        ls = ls + lx[8 * t : 8 * t + 8, :]
    ap[6, U : U + 8, :] = ls
    ap[7, U : U + 8, :] = ls

    def ay_copy(to):
        return copy(ap.at[to], ay.at[y], ay_s.at[to], ay_r.at[y], at_y(to))

    for k in (4, 3, 5, 2, 6, 1, 7):
        ay_copy(lax.rem(y + k, NY)).start()
    s = ap[y]
    for k in range(1, NY):
        src = lax.rem(y + k, NY)
        copy(ap.at[0], ay.at[src], ay_s.at[0], ay_r.at[src], other).wait_recv()
        s = s + ay[src]
    a[...] = s
    az_copy = copy(a, az, az_s, az_r, at_z(lax.rem(z + NT, NZ)))
    az_copy.start()
    az_copy.wait()
    ag[y] = s + az[...]

    def ag_copy(to):
        return copy(ag.at[y], ag.at[y], ag_s.at[to], ag_r.at[y], at_y(to))

    for k in (4, 3, 5, 2, 6, 1, 7):
        ag_copy(lax.rem(y + k, NY)).start()
    for k in range(1, NY):
        src = lax.rem(y + k, NY)
        copy(ag.at[0], ag.at[src], ag_s.at[0], ag_r.at[src], other).wait_recv()
    for k in range(NY):
        out[c, rows(x), 128 * k : 128 * (k + 1)] = ag[k, 0:U, :]
    for k in range(6):
        out[c, pl.ds(pl.multiple_of(x * U + 8 * k, 8), 8), 1024:1152] = ag[k, U : U + 8, :]

    def o_copy(k):
        xx, dev = at_x(k)
        blk = out.at[c, rows(x)]
        return copy(blk, blk, o_s.at[xx], o_r.at[x], dev)

    def oc_copy(xx, m):
        blk = out.at[m, rows(xx)]
        return copy(blk, blk, oc_s.at[xx], oc_r.at[xx], other)

    for k in (2, 1, 3):
        o_copy(k).start()
    oc_copy(x, c).start()
    for k in range(1, NX):
        xx = lax.rem(x + k, NX)
        blk = out.at[c, rows(xx)]
        copy(blk, blk, o_s.at[0], o_r.at[xx], other).wait_recv()
        oc_copy(xx, c).start()
    loss_out[...] = jnp.broadcast_to(
        jnp.sum(ag[6, U : U + 8, :], keepdims=True) * (1.0 / (NX * NY * NZ * U)), (8, 128)
    )
    for xx in range(NX):
        oc_copy(xx, 1 - c).wait_recv()

    for k in range(1, NT):
        to = lax.rem(zl + k, NT)
        part_copy(to).wait_send()
        d_copy(to).wait_send()
        lt_copy(to).wait_send()

    @pl.when(c == 0)
    def _():
        img_up(z).wait_send()
        img_down(z).wait_send()
        for s in range(1, 6):
            img_up(lax.rem(z + NZ - s, NZ)).wait_send()
            if s < 5:
                img_down(lax.rem(z + s, NZ)).wait_send()
        for s in range(NZ):
            img_over(s).wait_send()

    @pl.when(jnp.logical_and(c == 1, half == 0))
    def _():
        txt_over().wait_send()

    @pl.when(half == c)
    def _():
        for k in range(1, NY):
            txt_y(lax.rem(y + k, NY)).wait_send()

    for yi in range(4):
        for k in range(1, NX):
            txt_x(yi, k).wait_send()
            xr_copy(yi, k).wait_send()

        @pl.when(4 * c + yi != y)
        def _():
            yr_copy(yi).wait_send()

    lc_copy().wait_send()
    for q in range(NZ // 2):
        gx_copy(q, 1 - c).wait_send()

        @pl.when(2 * q + c != z)
        def _():
            zs_copy(q).wait_send()

    @pl.when(jnp.logical_and(c == 1, lax.rem(z, 2) == 1))
    def _():
        gl_copy(0).wait_send()

    @pl.when(jnp.logical_and(c == 0, half == 0))
    def _():
        gl_copy(1).wait_send()

    for k in range(1, NX):
        ax_copy(k).wait_send()
        lx_copy(k).wait_send()
        o_copy(k).wait_send()
    for k in range(1, NY):
        to = lax.rem(y + k, NY)
        ay_copy(to).wait_send()
        ag_copy(to).wait_send()
    for xx in range(NX):
        oc_copy(xx, c).wait_send()


def on_device(
    image_features, text_features, image_head, text_head, caption_ids, logit_scale, logit_bias
):
    x, y, zh, zl, c = place()
    table = caption_ids.reshape(NY, NX, 2, 2, NT, 24)
    ids_i = lax.dynamic_slice(table, (y, x, 0, 0, 0, 0), (1, 1, 2, 2, NT, 24))
    ids_i = ids_i.reshape(2, 2, NT, 24).transpose(0, 2, 1, 3).reshape(NI, 1)
    ids_t = lax.dynamic_slice(table, (4 * c, 0, zh, 0, zl, 0), (4, NX, 1, 2, 1, 24)).reshape(1, NJ)
    vm = pl.BlockSpec(memory_space=pltpu.VMEM)
    sm = pl.BlockSpec(memory_space=pltpu.SMEM)
    dma = pltpu.SemaphoreType.DMA
    scratch = dict(
        h=((192, E), BF16), fx=((144, 192), BF16), fa=((NT * U, 192), BF16),
        part=((NT * U, E), F32), spart=((NT * U, E), BF16), rpart=((NT * U, E), BF16),
        unit=((U, E), F32), inv=((U, 128), F32),
        img=((NI, E), BF16), txt=((NJ, E), BF16), own=((U, E), BF16),
        ip=((NI, NJ), F32), coef=((NI, NJ), BF16), gi=((NI, E), F32), gt=((NJ, E), F32),
        gix=((NI // 2, E), F32), zs=((NI // 2, E), BF16), zr=((NI, E), BF16),
        gtb=((NJ, E), BF16), xr=((NJ, E), BF16), ys=((4 * U, E), BF16), yr=((NY * U, E), BF16),
        gsum=((2, U, E), F32), gland=((U, E), F32),
        delta=((NT * U, E), BF16), g=((192, E), F32), ax=((192, E), F32),
        a=((U + 8, 128), F32), ap=((NY, U + 8, 128), F32), ay=((NY, U + 8, 128), F32),
        az=((U + 8, 128), F32), ag=((NY, U + 8, 128), F32),
        lp=((8, 128), F32), lc=((8, 128), F32), lt=((8 * NT, 128), F32), lx=((8 * NX, 128), F32),
    )
    sems = [
        (), (), (), (NT,), (NT,), (2, NZ), (NZ,), (NZ,), (NZ,), (), (), (NY,), (4,), (4, NX), (4, NX),
        (6,), (6,), (6,), (NZ,), (4, NX), (4, NX), (4,), (NY,), (), (), (NT,), (NT,),
        (NX,), (NX,), (NY,), (NY,), (), (), (NY,), (NY,), (NX,), (NX,), (NX,), (NX,),
        (), (), (NT,), (NT,), (NX,), (NX,),
    ]
    out, loss = pl.pallas_call(
        kernel,
        out_shape=(
            jax.ShapeDtypeStruct((2, 192, E), F32),
            jax.ShapeDtypeStruct((8, 128), F32),
        ),
        in_specs=[
            vm, vm, pl.BlockSpec(memory_space=pl.ANY), pl.BlockSpec(memory_space=pl.ANY),
            vm, vm, sm, sm,
        ],
        out_specs=(vm, vm),
        scratch_shapes=[pltpu.VMEM(*scratch[n]) for n in scratch]
        + [dma(s) if s else dma for s in sems],
        compiler_params=pltpu.CompilerParams(
            collective_id=0, has_side_effects=True, vmem_limit_bytes=56 * 2**20
        ),
        cost_estimate=pl.CostEstimate(
            flops=4 * 10**9, bytes_accessed=10**7, transcendentals=10**6
        ),
        name="siglip",
    )(
        image_features, text_features, image_head, text_head, ids_i, ids_t, logit_scale, logit_bias
    )
    return loss[0, :1], out[0], out[1]


def solution(mesh):
    placed = (
        P("batch", "tower"),
        P("batch", "tower"),
        P("tower", None),
        P("tower", None),
        P(),
        P(),
        P(),
    )
    return jax.shard_map(
        on_device,
        mesh=mesh,
        in_specs=placed,
        out_specs=(P(), P("tower", None), P("tower", None)),
        check_vma=False,
    )
```

```python
import functools

import jax
import jax.numpy as jnp
from jax import lax
from jax.experimental import pallas as pl
from jax.experimental.pallas import tpu as pltpu
from jax.sharding import PartitionSpec as P

MESH = pl.DeviceIdType.MESH
F32, BF16 = jnp.float32, jnp.bfloat16
NX, NY, NZ, NT = 4, 8, 12, 6
E = 1152
U = 48
NP = 3
NI, NJ = NZ * U, 4 * NX * U
norm_eps = 1e-06


def place():
    b = lax.axis_index("batch")
    zl = lax.axis_index("tower")
    c = lax.rem(b, 2)
    zh = lax.rem(b // 2, 2)
    x = lax.rem(b // 4, NX)
    y = b // 16
    return x, y, zh, zl, c


def device(x, y, z, c):
    return (((y * NX + x) * 2 + z // NT) * 2 + c, lax.rem(z, NT))


def rows(i, n=U):
    return pl.ds(pl.multiple_of(i * n, 8 if n % 16 else 16), n)


def copy(src, dst, ss, rs, dev):
    return pltpu.make_async_remote_copy(
        src_ref=src, dst_ref=dst, send_sem=ss, recv_sem=rs, device_id=dev, device_id_type=MESH
    )


def kernel(
    fi, ft, hi, ht, ids_i, ids_t, scale, bias,
    out_i, out_t, loss_out,
    h, fx, fa, part, spart, rpart, unit, inv,
    img, txt, own, ip, coef, gi, gt, gix, zs, zr, gtb, xr, ys, yr, gsum, gland,
    delta, g, gb, ax, ob, a, ap, ay, az, ag, lp, lc, lt, lx,
    hsem, fs, fr, ps, pr, isn, irc, ic_s, ic_r, ts_s, ts_r, ys_s, ys_r, xs_s, xs_r,
    gx_s, gx_r, zs_s, zs_r, xr_s, xr_r, yr_s, yr_r, gl_s, gl_r, d_s, d_r,
    ax_s, ax_r, ay_s, ay_r, az_s, az_r, ag_s, ag_r, o_s, o_r, oc_s, oc_r,
    lc_s, lc_r, lt_s, lt_r, lx_s, lx_r,
):
    x, y, zh, zl, c = place()
    z = zh * NT + zl
    other = device(x, y, z, 1 - c)
    half = y // 4

    def at_x(k):
        xx = lax.rem(x + k, NX)
        return xx, device(xx, y, z, c)

    def at_y(yy):
        return device(x, yy, z, c)

    def at_z(zz):
        return device(x, y, zz, c)

    @pl.when(c == 0)
    def _():
        pltpu.make_async_copy(hi, h, hsem).start()

    @pl.when(c == 1)
    def _():
        pltpu.make_async_copy(ht, h, hsem).start()

    barrier = pltpu.get_barrier_semaphore()

    def greet(dev):
        pl.semaphore_signal(barrier, inc=1, device_id=dev, device_id_type=MESH)

    greet(other)
    for k in range(1, NX):
        greet(at_x(k)[1])
    for k in range(1, NY):
        greet(at_y(lax.rem(y + k, NY)))
    for k in range(1, NZ):
        greet(at_z(lax.rem(z + k, NZ)))
    pl.semaphore_wait(barrier, 1 + NX - 1 + NY - 1 + NZ - 1)

    @pl.when(c == 0)
    def _():
        copy(ft, fx, fs, fr, other).start()

    @pl.when(c == 1)
    def _():
        copy(fi, fx, fs, fr, other).start()

    copy(ft, fx, fs, fr, other).wait()

    def gather_features(first, second):
        fst = first[...].astype(F32)
        snd = second[...].astype(F32)
        for t in range(NT):
            fa[t * U : (t + 1) * U, :] = jnp.concatenate(
                [fst[24 * t : 24 * t + 24], snd[24 * t : 24 * t + 24]], axis=0
            ).astype(BF16)

    @pl.when(c == 0)
    def _():
        gather_features(fi, fx)

    @pl.when(c == 1)
    def _():
        gather_features(fx, ft)

    pltpu.make_async_copy(hi, h, hsem).wait()

    def piece(d, p):
        return rows(d * NP + p, U // NP)

    part[...] = jnp.dot(fa[...], h[...], preferred_element_type=F32)
    spart[...] = part[...].astype(BF16)

    def part_copy(to):
        return copy(
            spart.at[rows(to)], rpart.at[rows(zl)], ps.at[to], pr.at[zl], at_z(zh * NT + to)
        )

    def part_wait(src):
        copy(spart.at[rows(0)], rpart.at[rows(src)], ps.at[0], pr.at[src], other).wait_recv()

    for k in range(1, NT):
        part_copy(lax.rem(zl + k, NT)).start()
    raw = part[rows(zl), :]
    for k in range(1, NT):
        src = lax.rem(zl + k, NT)
        part_wait(src)
        raw = raw + rpart[rows(src), :].astype(F32)
    inverse = lax.rsqrt(jnp.sum(raw * raw, axis=-1, keepdims=True) + norm_eps)
    raw = raw * inverse
    unit[...] = raw
    inv[...] = jnp.broadcast_to(inverse, (U, 128))
    own[...] = raw.astype(BF16)

    mine = rows(lax.rem(y, 4) * NX + x)

    def img_up(slot):
        return copy(
            img.at[rows(slot)], img.at[rows(slot)], isn.at[0, slot], irc.at[slot],
            at_z(lax.rem(z + 1, NZ)),
        )

    def img_down(slot):
        return copy(
            img.at[rows(slot)], img.at[rows(slot)], isn.at[1, slot], irc.at[slot],
            at_z(lax.rem(z + NZ - 1, NZ)),
        )

    def img_over(slot):
        return copy(
            img.at[rows(slot)], img.at[rows(slot)], ic_s.at[slot], ic_r.at[slot], other
        )

    def txt_over():
        return copy(own, txt.at[mine], ts_s, ts_r, other)

    def txt_y(to):
        return copy(txt.at[mine], txt.at[mine], ys_s.at[to], ys_r.at[lax.rem(y, 4)], at_y(to))

    def txt_x(yi, k):
        xx, dev = at_x(k)
        slot = rows(yi * NX + x)
        return copy(txt.at[slot], txt.at[slot], xs_s.at[yi, xx], xs_r.at[yi, x], dev)

    def txt_y_send():
        for k in (4, 3, 5, 2, 6, 1, 7):
            txt_y(lax.rem(y + k, NY)).start()

    def txt_forward(k):
        yi = lax.rem(y + k, 4)

        @pl.when(4 * c + yi != y)
        def _():
            slot = rows(yi * NX + x)
            copy(txt.at[slot], txt.at[slot], ys_s.at[0], ys_r.at[yi], other).wait_recv()

        for kx in (2, 1, 3):
            txt_x(yi, kx).start()

    @pl.when(c == 1)
    def _():
        @pl.when(half == 0)
        def _():
            txt_over().start()

        @pl.when(half == 1)
        def _():
            txt[mine, :] = own[...]
            txt_y_send()

        for k in range(4):
            txt_forward(k)
        for s in range(NZ):
            img_over(s).wait_recv()

    @pl.when(c == 0)
    def _():
        img[rows(z), :] = own[...]
        img_up(z).start()
        img_down(z).start()
        img_over(z).start()

        @pl.when(half == 0)
        def _():
            txt_over().wait_recv()
            txt_y_send()

        for s in range(1, 7):
            lo = lax.rem(z + NZ - s, NZ)
            hi_ = lax.rem(z + s, NZ)
            img_up(lo).wait_recv()
            if s < 6:
                img_up(lo).start()
            img_over(lo).start()
            if s < 6:
                img_down(hi_).wait_recv()
                if s < 5:
                    img_down(hi_).start()
                img_over(hi_).start()
            if s <= 4:
                txt_forward(s - 1)

    for yi in range(4):
        for k in range(1, NX):
            xx = lax.rem(x + k, NX)
            slot = rows(yi * NX + xx)
            copy(txt.at[slot], txt.at[slot], xs_s.at[0, 0], xs_r.at[yi, xx], other).wait_recv()

    ip[...] = lax.dot_general(
        img[...], txt[...], (((1,), (1,)), ((), ())), preferred_element_type=F32
    )
    mult, shift = scale[0], bias[0]
    factor = mult * (1.0 / (NX * NY * NZ * U))

    def pairs(i, total):
        r = rows(i)
        logits = mult * ip[r, :] + shift
        same = ids_i[r, :] == ids_t[...]
        v = jnp.where(same, logits, -logits)
        e = jnp.exp(-jnp.abs(v))
        d = 1.0 / (1.0 + e)
        sig = jnp.where(v >= 0, e * d, d)
        coef[r, :] = (jnp.where(same, -factor, factor) * sig).astype(BF16)
        ls = jnp.log1p(e) - jnp.minimum(v, 0.0)
        ls = jnp.sum(ls.reshape(U // 8, 8, NJ), axis=0)
        for j in range(NJ // 128):
            total = total + ls[:, 128 * j : 128 * (j + 1)]
        return total

    lp[...] = lax.fori_loop(0, NZ, pairs, jnp.zeros((8, 128), F32))

    def lc_copy():
        return copy(lp, lc, lc_s, lc_r, other)

    lc_copy().start()

    def gx_copy(q, to_core):
        return copy(gi.at[rows(2 * q + to_core)], gix.at[rows(q)], gx_s.at[q], gx_r.at[q], other)

    def xr_copy(yi, k):
        xx, dev = at_x(k)
        return copy(
            gtb.at[rows(yi * NX + xx)], xr.at[rows(yi * NX + x)], xr_s.at[yi, xx], xr_r.at[yi, x],
            dev,
        )

    for jb in range(2):
        blk = slice(jb * NJ // 2, (jb + 1) * NJ // 2)
        gt[blk, :] = lax.dot_general(
            coef[:, blk], img[...], (((0,), (0,)), ((), ())), preferred_element_type=F32
        )
        gtb[blk, :] = gt[blk, :].astype(BF16)
        for yi in (2 * jb, 2 * jb + 1):
            for kx in (2, 1, 3):
                xr_copy(yi, kx).start()

    for ib in range(3):
        blk = slice(ib * NI // 3, (ib + 1) * NI // 3)
        gi[blk, :] = jnp.dot(coef[blk, :], txt[...], preferred_element_type=F32)
        for q in (2 * ib, 2 * ib + 1):
            gx_copy(q, 1 - c).start()

    lc_copy().wait_recv()
    lt[rows(zl, 8), :] = lp[...] + lc[...]

    def lt_copy(to):
        return copy(
            lt.at[rows(zl, 8)], lt.at[rows(zl, 8)], lt_s.at[to], lt_r.at[zl], at_z(zh * NT + to)
        )

    for k in range(1, NT):
        lt_copy(lax.rem(zl + k, NT)).start()

    def zs_copy(q):
        to = 2 * q + c
        return copy(zs.at[rows(q)], zr.at[rows(z)], zs_s.at[q], zr_r.at[z], at_z(to))

    zr_r = zs_r
    for k in range(NZ // 2):
        q = k
        gx_copy(q, c).wait_recv()
        to = 2 * q + c
        s = gi[rows(to), :] + gix[rows(q), :]
        zs[rows(q), :] = s.astype(BF16)

        @pl.when(to != z)
        def _():
            zs_copy(q).start()

        @pl.when(to == z)
        def _():
            gsum[0] = s

    def yr_copy(yi):
        to = 4 * c + yi
        return copy(ys.at[rows(yi)], yr.at[rows(y)], yr_s.at[yi], yr_r.at[y], at_y(to))

    for yi in range(4):
        s = gt[rows(yi * NX + x), :]
        for kx in range(1, NX):
            xx = lax.rem(x + kx, NX)
            slot = rows(yi * NX + xx)
            copy(gtb.at[slot], xr.at[slot], xr_s.at[0, 0], xr_r.at[yi, xx], other).wait_recv()
            s = s + xr[slot, :].astype(F32)
        ys[rows(yi), :] = s.astype(BF16)

        @pl.when(4 * c + yi != y)
        def _():
            yr_copy(yi).start()

        @pl.when(4 * c + yi == y)
        def _():
            gsum[1] = s

    def gl_copy(m):
        return copy(gsum.at[m], gland, gl_s, gl_r, other)

    @pl.when(lax.rem(z, 2) == c)
    def _():
        s = gsum[0]
        for k in range(1, NZ):
            src = lax.rem(z + k, NZ)
            copy(zs.at[rows(0)], zr.at[rows(src)], zs_s.at[0], zr_r.at[src], other).wait_recv()
            s = s + zr[rows(src), :].astype(F32)
        gsum[0] = s

        @pl.when(c == 1)
        def _():
            gl_copy(0).start()

    @pl.when(half == c)
    def _():
        s = gsum[1]
        for k in range(1, NY):
            src = lax.rem(y + k, NY)
            copy(ys.at[rows(0)], yr.at[rows(src)], yr_s.at[0], yr_r.at[src], other).wait_recv()
            s = s + yr[rows(src), :].astype(F32)
        gsum[1] = s

        @pl.when(c == 0)
        def _():
            gl_copy(1).start()

    @pl.when(jnp.logical_and(c == 0, lax.rem(z, 2) == 1))
    def _():
        gl_copy(0).wait_recv()
        gsum[0] = gland[...]

    @pl.when(jnp.logical_and(c == 1, half == 0))
    def _():
        gl_copy(0).wait_recv()
        gsum[1] = gland[...]

    grad = gsum[c]
    un = unit[...]
    dl = inv[:, 0:1] * (grad - un * jnp.sum(un * grad, axis=-1, keepdims=True))
    delta[rows(zl), :] = dl.astype(BF16)

    def d_copy(src, p, right):
        blk = piece(src, p)
        i = src * NP + p
        dev = at_z(lax.rem(z + (1 if right else NZ - 1), NZ))
        return copy(delta.at[blk], delta.at[blk], d_s.at[0 if right else 1, i], d_r.at[i], dev)

    def d_step(src, p, right):
        @pl.when(zl != (NT - 1 if right else 0))
        def _():
            d_copy(src, p, right).start()

    def d_wait(src, p):
        d_copy(src, p, True).wait_recv()

    for p in range(NP):
        d_step(zl, p, True)
        d_step(zl, p, False)
    for k in range(1, NT):
        for p in range(NP):

            @pl.when(zl >= k)
            def _():
                d_wait(zl - k, p)
                d_step(zl - k, p, True)

            @pl.when(zl + k < NT)
            def _():
                d_wait(zl + k, p)
                d_step(zl + k, p, False)

    for k in range(1, NT):
        src = lax.rem(zl + k, NT)
        copy(lt.at[rows(0, 8)], lt.at[rows(src, 8)], lt_s.at[0], lt_r.at[src], other).wait_recv()
    ls = lt[0:8, :]
    for t in range(1, NT):
        ls = ls + lt[8 * t : 8 * t + 8, :]
    lx[rows(x, 8), :] = ls

    g[...] = lax.dot_general(
        fa[...], delta[...], (((0,), (0,)), ((), ())), preferred_element_type=F32
    )

    gb[...] = g[...].astype(BF16)

    def ax_copy(k):
        xx, dev = at_x(k)
        return copy(gb.at[rows(xx)], ax.at[rows(x)], ax_s.at[xx], ax_r.at[x], dev)

    def lx_copy(k):
        xx, dev = at_x(k)
        return copy(lx.at[rows(x, 8)], lx.at[rows(x, 8)], lx_s.at[xx], lx_r.at[x], dev)

    for k in (2, 1, 3):
        ax_copy(k).start()
        lx_copy(k).start()
    s = g[rows(x), :]
    for k in range(1, NX):
        xx = lax.rem(x + k, NX)
        copy(gb.at[rows(0)], ax.at[rows(xx)], ax_s.at[0], ax_r.at[xx], other).wait_recv()
        s = s + ax[rows(xx), :].astype(F32)
        copy(lx.at[rows(0, 8)], lx.at[rows(xx, 8)], lx_s.at[0], lx_r.at[xx], other).wait_recv()
    for k in range(NY):
        ap[k, 0:U, :] = s[:, 128 * k : 128 * (k + 1)]
    for k in range(6):
        ap[k, U : U + 8, :] = s[8 * k : 8 * k + 8, 1024:1152]
    ls = lx[0:8, :]
    for t in range(1, NX):
        ls = ls + lx[8 * t : 8 * t + 8, :]
    ap[6, U : U + 8, :] = ls
    ap[7, U : U + 8, :] = ls

    def ay_copy(to):
        return copy(ap.at[to], ay.at[y], ay_s.at[to], ay_r.at[y], at_y(to))

    for k in (4, 3, 5, 2, 6, 1, 7):
        ay_copy(lax.rem(y + k, NY)).start()
    s = ap[y]
    for k in range(1, NY):
        src = lax.rem(y + k, NY)
        copy(ap.at[0], ay.at[src], ay_s.at[0], ay_r.at[src], other).wait_recv()
        s = s + ay[src]
    a[...] = s
    az_copy = copy(a, az, az_s, az_r, at_z(lax.rem(z + NT, NZ)))
    az_copy.start()
    az_copy.wait()
    ag[y] = s + az[...]

    def ag_copy(to):
        return copy(ag.at[y], ag.at[y], ag_s.at[to], ag_r.at[y], at_y(to))

    for k in (4, 3, 5, 2, 6, 1, 7):
        ag_copy(lax.rem(y + k, NY)).start()
    for k in range(1, NY):
        src = lax.rem(y + k, NY)
        copy(ag.at[0], ag.at[src], ag_s.at[0], ag_r.at[src], other).wait_recv()
    last = jnp.concatenate([ag[k, U : U + 8, :] for k in range(6)], axis=0)
    ob[c, rows(x), :] = jnp.concatenate(
        [ag[k, 0:U, :] for k in range(NY)] + [last], axis=1
    ).astype(BF16)

    def o_copy(k):
        xx, dev = at_x(k)
        blk = ob.at[c, rows(x)]
        return copy(blk, blk, o_s.at[xx], o_r.at[x], dev)

    def oc_copy(xx, m):
        blk = ob.at[m, rows(xx)]
        return copy(blk, blk, oc_s.at[xx], oc_r.at[xx], other)

    for k in (2, 1, 3):
        o_copy(k).start()
    oc_copy(x, c).start()
    for k in range(1, NX):
        xx = lax.rem(x + k, NX)
        blk = ob.at[c, rows(xx)]
        copy(blk, blk, o_s.at[0], o_r.at[xx], other).wait_recv()
        oc_copy(xx, c).start()
    loss_out[0] = jnp.sum(ag[6, U : U + 8, :]) * (1.0 / (NX * NY * NZ * U))
    for xx in range(NX):
        oc_copy(xx, 1 - c).wait_recv()
    out_i[...] = ob[0].astype(F32)
    out_t[...] = ob[1].astype(F32)

    for k in range(1, NT):
        to = lax.rem(zl + k, NT)
        part_copy(to).wait_send()
        lt_copy(to).wait_send()
    for d in range(NT):
        for p in range(NP):

            @pl.when(jnp.logical_and(d <= zl, zl != NT - 1))
            def _():
                d_copy(d, p, True).wait_send()

            @pl.when(jnp.logical_and(d >= zl, zl != 0))
            def _():
                d_copy(d, p, False).wait_send()

    @pl.when(c == 0)
    def _():
        img_up(z).wait_send()
        img_down(z).wait_send()
        for s in range(1, 6):
            img_up(lax.rem(z + NZ - s, NZ)).wait_send()
            if s < 5:
                img_down(lax.rem(z + s, NZ)).wait_send()
        for s in range(NZ):
            img_over(s).wait_send()

    @pl.when(jnp.logical_and(c == 1, half == 0))
    def _():
        txt_over().wait_send()

    @pl.when(half == c)
    def _():
        for k in range(1, NY):
            txt_y(lax.rem(y + k, NY)).wait_send()

    for yi in range(4):
        for k in range(1, NX):
            txt_x(yi, k).wait_send()
            xr_copy(yi, k).wait_send()

        @pl.when(4 * c + yi != y)
        def _():
            yr_copy(yi).wait_send()

    lc_copy().wait_send()
    for q in range(NZ // 2):
        gx_copy(q, 1 - c).wait_send()

        @pl.when(2 * q + c != z)
        def _():
            zs_copy(q).wait_send()

    @pl.when(jnp.logical_and(c == 1, lax.rem(z, 2) == 1))
    def _():
        gl_copy(0).wait_send()

    @pl.when(jnp.logical_and(c == 0, half == 0))
    def _():
        gl_copy(1).wait_send()

    for k in range(1, NX):
        ax_copy(k).wait_send()
        lx_copy(k).wait_send()
        o_copy(k).wait_send()
    for k in range(1, NY):
        to = lax.rem(y + k, NY)
        ay_copy(to).wait_send()
        ag_copy(to).wait_send()
    for xx in range(NX):
        oc_copy(xx, c).wait_send()


def on_device(
    image_features, text_features, image_head, text_head, caption_ids, logit_scale, logit_bias
):
    x, y, zh, zl, c = place()
    table = caption_ids.reshape(NY, NX, 2, 2, NT, 24)
    ids_i = lax.dynamic_slice(table, (y, x, 0, 0, 0, 0), (1, 1, 2, 2, NT, 24))
    ids_i = ids_i.reshape(2, 2, NT, 24).transpose(0, 2, 1, 3).reshape(NI, 1)
    ids_t = lax.dynamic_slice(table, (4 * c, 0, zh, 0, zl, 0), (4, NX, 1, 2, 1, 24)).reshape(1, NJ)
    vm = pl.BlockSpec(memory_space=pltpu.VMEM)
    sm = pl.BlockSpec(memory_space=pltpu.SMEM)
    dma = pltpu.SemaphoreType.DMA
    scratch = dict(
        h=((192, E), BF16), fx=((144, 192), BF16), fa=((NT * U, 192), BF16),
        part=((NT * U, E), F32), spart=((NT * U, E), BF16), rpart=((NT * U, E), BF16),
        unit=((U, E), F32), inv=((U, 128), F32),
        img=((NI, E), BF16), txt=((NJ, E), BF16), own=((U, E), BF16),
        ip=((NI, NJ), F32), coef=((NI, NJ), BF16), gi=((NI, E), F32), gt=((NJ, E), F32),
        gix=((NI // 2, E), F32), zs=((NI // 2, E), BF16), zr=((NI, E), BF16),
        gtb=((NJ, E), BF16), xr=((NJ, E), BF16), ys=((4 * U, E), BF16), yr=((NY * U, E), BF16),
        gsum=((2, U, E), F32), gland=((U, E), F32),
        delta=((NT * U, E), BF16), g=((192, E), F32), gb=((192, E), BF16), ax=((192, E), BF16),
        ob=((2, 192, E), BF16),
        a=((U + 8, 128), F32), ap=((NY, U + 8, 128), F32), ay=((NY, U + 8, 128), F32),
        az=((U + 8, 128), F32), ag=((NY, U + 8, 128), F32),
        lp=((8, 128), F32), lc=((8, 128), F32), lt=((8 * NT, 128), F32), lx=((8 * NX, 128), F32),
    )
    sems = [
        (), (), (), (NT,), (NT,), (2, NZ), (NZ,), (NZ,), (NZ,), (), (), (NY,), (4,), (4, NX), (4, NX),
        (6,), (6,), (6,), (NZ,), (4, NX), (4, NX), (4,), (NY,), (), (), (2, NT * NP), (NT * NP,),
        (NX,), (NX,), (NY,), (NY,), (), (), (NY,), (NY,), (NX,), (NX,), (NX,), (NX,),
        (), (), (NT,), (NT,), (NX,), (NX,),
    ]
    out_i, out_t, loss = pl.pallas_call(
        kernel,
        out_shape=(
            jax.ShapeDtypeStruct((192, E), F32),
            jax.ShapeDtypeStruct((192, E), F32),
            jax.ShapeDtypeStruct((1,), F32),
        ),
        in_specs=[
            vm, vm, pl.BlockSpec(memory_space=pl.ANY), pl.BlockSpec(memory_space=pl.ANY),
            vm, vm, sm, sm,
        ],
        out_specs=(vm, vm, sm),
        scratch_shapes=[pltpu.VMEM(*scratch[n]) for n in scratch]
        + [dma(s) if s else dma for s in sems],
        compiler_params=pltpu.CompilerParams(
            collective_id=0, has_side_effects=True, vmem_limit_bytes=56 * 2**20
        ),
        cost_estimate=pl.CostEstimate(
            flops=4 * 10**9, bytes_accessed=10**7, transcendentals=10**6
        ),
        name="siglip",
    )(
        image_features, text_features, image_head, text_head, ids_i, ids_t, logit_scale, logit_bias
    )
    return loss, out_i, out_t


def solution(mesh):
    placed = (
        P("batch", "tower"),
        P("batch", "tower"),
        P("tower", None),
        P("tower", None),
        P(),
        P(),
        P(),
    )
    return jax.shard_map(
        on_device,
        mesh=mesh,
        in_specs=placed,
        out_specs=(P(), P("tower", None), P("tower", None)),
        check_vma=False,
    )
```

```python
import functools

import jax
import jax.numpy as jnp
from jax import lax
from jax.experimental import pallas as pl
from jax.experimental.pallas import tpu as pltpu
from jax.sharding import PartitionSpec as P

MESH = pl.DeviceIdType.MESH
F32, BF16 = jnp.float32, jnp.bfloat16
NX, NY, NZ, NT = 4, 8, 12, 6
E = 1152
U = 48
NP = 3
NI, NJ = NZ * U, 4 * NX * U
norm_eps = 1e-06


def place():
    b = lax.axis_index("batch")
    zl = lax.axis_index("tower")
    c = lax.rem(b, 2)
    zh = lax.rem(b // 2, 2)
    x = lax.rem(b // 4, NX)
    y = b // 16
    return x, y, zh, zl, c


def device(x, y, z, c):
    return (((y * NX + x) * 2 + z // NT) * 2 + c, lax.rem(z, NT))


def rows(i, n=U):
    return pl.ds(pl.multiple_of(i * n, 8 if n % 16 else 16), n)


def copy(src, dst, ss, rs, dev):
    return pltpu.make_async_remote_copy(
        src_ref=src, dst_ref=dst, send_sem=ss, recv_sem=rs, device_id=dev, device_id_type=MESH
    )


def kernel(
    fi, ft, hi, ht, ids_i, ids_t, scale, bias,
    ob, loss_out,
    h, fx, fa, part, spart, rpart, unit, inv,
    img, txt, own, ip, coef, gi, gt, gix, zs, zr, gtb, xr, ys, yr, gsum, gland,
    delta, g, gb, ax, a, ap, ay, az, ag, lp, lc, lt, lx,
    hsem, fs, fr, ps, pr, isn, irc, ic_s, ic_r, ts_s, ts_r, ys_s, ys_r, xs_s, xs_r,
    gx_s, gx_r, zs_s, zs_r, xr_s, xr_r, yr_s, yr_r, gl_s, gl_r, d_s, d_r,
    ax_s, ax_r, ay_s, ay_r, az_s, az_r, ag_s, ag_r, o_s, o_r, oc_s, oc_r,
    lc_s, lc_r, lt_s, lt_r, lx_s, lx_r,
):
    x, y, zh, zl, c = place()
    z = zh * NT + zl
    other = device(x, y, z, 1 - c)
    half = y // 4

    def at_x(k):
        xx = lax.rem(x + k, NX)
        return xx, device(xx, y, z, c)

    def at_y(yy):
        return device(x, yy, z, c)

    def at_z(zz):
        return device(x, y, zz, c)

    @pl.when(c == 0)
    def _():
        pltpu.make_async_copy(hi, h, hsem).start()

    @pl.when(c == 1)
    def _():
        pltpu.make_async_copy(ht, h, hsem).start()

    barrier = pltpu.get_barrier_semaphore()

    def greet(dev):
        pl.semaphore_signal(barrier, inc=1, device_id=dev, device_id_type=MESH)

    greet(other)
    for k in range(1, NX):
        greet(at_x(k)[1])
    for k in range(1, NY):
        greet(at_y(lax.rem(y + k, NY)))
    for k in range(1, NZ):
        greet(at_z(lax.rem(z + k, NZ)))
    pl.semaphore_wait(barrier, 1 + NX - 1 + NY - 1 + NZ - 1)

    @pl.when(c == 0)
    def _():
        copy(ft, fx, fs, fr, other).start()

    @pl.when(c == 1)
    def _():
        copy(fi, fx, fs, fr, other).start()

    copy(ft, fx, fs, fr, other).wait()

    def gather_features(first, second):
        fst = first[...].astype(F32)
        snd = second[...].astype(F32)
        for t in range(NT):
            fa[t * U : (t + 1) * U, :] = jnp.concatenate(
                [fst[24 * t : 24 * t + 24], snd[24 * t : 24 * t + 24]], axis=0
            ).astype(BF16)

    @pl.when(c == 0)
    def _():
        gather_features(fi, fx)

    @pl.when(c == 1)
    def _():
        gather_features(fx, ft)

    pltpu.make_async_copy(hi, h, hsem).wait()

    def piece(d, p):
        return rows(d * NP + p, U // NP)

    part[...] = jnp.dot(fa[...], h[...], preferred_element_type=F32)
    spart[...] = part[...].astype(BF16)

    def part_copy(to):
        return copy(
            spart.at[rows(to)], rpart.at[rows(zl)], ps.at[to], pr.at[zl], at_z(zh * NT + to)
        )

    def part_wait(src):
        copy(spart.at[rows(0)], rpart.at[rows(src)], ps.at[0], pr.at[src], other).wait_recv()

    for k in range(1, NT):
        part_copy(lax.rem(zl + k, NT)).start()
    raw = part[rows(zl), :]
    for k in range(1, NT):
        src = lax.rem(zl + k, NT)
        part_wait(src)
        raw = raw + rpart[rows(src), :].astype(F32)
    inverse = lax.rsqrt(jnp.sum(raw * raw, axis=-1, keepdims=True) + norm_eps)
    raw = raw * inverse
    unit[...] = raw
    inv[...] = jnp.broadcast_to(inverse, (U, 128))
    own[...] = raw.astype(BF16)

    mine = rows(lax.rem(y, 4) * NX + x)

    def img_up(slot):
        return copy(
            img.at[rows(slot)], img.at[rows(slot)], isn.at[0, slot], irc.at[slot],
            at_z(lax.rem(z + 1, NZ)),
        )

    def img_down(slot):
        return copy(
            img.at[rows(slot)], img.at[rows(slot)], isn.at[1, slot], irc.at[slot],
            at_z(lax.rem(z + NZ - 1, NZ)),
        )

    def img_over(slot):
        return copy(
            img.at[rows(slot)], img.at[rows(slot)], ic_s.at[slot], ic_r.at[slot], other
        )

    def txt_over():
        return copy(own, txt.at[mine], ts_s, ts_r, other)

    def txt_y(to):
        return copy(txt.at[mine], txt.at[mine], ys_s.at[to], ys_r.at[lax.rem(y, 4)], at_y(to))

    def txt_x(yi, k):
        xx, dev = at_x(k)
        slot = rows(yi * NX + x)
        return copy(txt.at[slot], txt.at[slot], xs_s.at[yi, xx], xs_r.at[yi, x], dev)

    def txt_y_send():
        for k in (4, 3, 5, 2, 6, 1, 7):
            txt_y(lax.rem(y + k, NY)).start()

    def txt_forward(k):
        yi = lax.rem(y + k, 4)

        @pl.when(4 * c + yi != y)
        def _():
            slot = rows(yi * NX + x)
            copy(txt.at[slot], txt.at[slot], ys_s.at[0], ys_r.at[yi], other).wait_recv()

        for kx in (2, 1, 3):
            txt_x(yi, kx).start()

    @pl.when(c == 1)
    def _():
        @pl.when(half == 0)
        def _():
            txt_over().start()

        @pl.when(half == 1)
        def _():
            txt[mine, :] = own[...]
            txt_y_send()

        for k in range(4):
            txt_forward(k)
        for s in range(NZ):
            img_over(s).wait_recv()

    @pl.when(c == 0)
    def _():
        img[rows(z), :] = own[...]
        img_up(z).start()
        img_down(z).start()
        img_over(z).start()

        @pl.when(half == 0)
        def _():
            txt_over().wait_recv()
            txt_y_send()

        for s in range(1, 7):
            lo = lax.rem(z + NZ - s, NZ)
            hi_ = lax.rem(z + s, NZ)
            img_up(lo).wait_recv()
            if s < 6:
                img_up(lo).start()
            img_over(lo).start()
            if s < 6:
                img_down(hi_).wait_recv()
                if s < 5:
                    img_down(hi_).start()
                img_over(hi_).start()
            if s <= 4:
                txt_forward(s - 1)

    for yi in range(4):
        for k in range(1, NX):
            xx = lax.rem(x + k, NX)
            slot = rows(yi * NX + xx)
            copy(txt.at[slot], txt.at[slot], xs_s.at[0, 0], xs_r.at[yi, xx], other).wait_recv()

    ip[...] = lax.dot_general(
        img[...], txt[...], (((1,), (1,)), ((), ())), preferred_element_type=F32
    )
    mult, shift = scale[0], bias[0]
    factor = mult * (1.0 / (NX * NY * NZ * U))

    def pairs(i, total):
        r = rows(i)
        logits = mult * ip[r, :] + shift
        same = ids_i[r, :] == ids_t[...]
        v = jnp.where(same, logits, -logits)
        e = jnp.exp(-jnp.abs(v))
        d = 1.0 / (1.0 + e)
        sig = jnp.where(v >= 0, e * d, d)
        coef[r, :] = (jnp.where(same, -factor, factor) * sig).astype(BF16)
        ls = jnp.log1p(e) - jnp.minimum(v, 0.0)
        ls = jnp.sum(ls.reshape(U // 8, 8, NJ), axis=0)
        for j in range(NJ // 128):
            total = total + ls[:, 128 * j : 128 * (j + 1)]
        return total

    lp[...] = lax.fori_loop(0, NZ, pairs, jnp.zeros((8, 128), F32))

    def lc_copy():
        return copy(lp, lc, lc_s, lc_r, other)

    lc_copy().start()

    def gx_copy(q, to_core):
        return copy(gi.at[rows(2 * q + to_core)], gix.at[rows(q)], gx_s.at[q], gx_r.at[q], other)

    def xr_copy(yi, k):
        xx, dev = at_x(k)
        return copy(
            gtb.at[rows(yi * NX + xx)], xr.at[rows(yi * NX + x)], xr_s.at[yi, xx], xr_r.at[yi, x],
            dev,
        )

    for jb in range(2):
        blk = slice(jb * NJ // 2, (jb + 1) * NJ // 2)
        gt[blk, :] = lax.dot_general(
            coef[:, blk], img[...], (((0,), (0,)), ((), ())), preferred_element_type=F32
        )
        gtb[blk, :] = gt[blk, :].astype(BF16)
        for yi in (2 * jb, 2 * jb + 1):
            for kx in (2, 1, 3):
                xr_copy(yi, kx).start()

    for ib in range(3):
        blk = slice(ib * NI // 3, (ib + 1) * NI // 3)
        gi[blk, :] = jnp.dot(coef[blk, :], txt[...], preferred_element_type=F32)
        for q in (2 * ib, 2 * ib + 1):
            gx_copy(q, 1 - c).start()

    lc_copy().wait_recv()
    lt[rows(zl, 8), :] = lp[...] + lc[...]

    def lt_copy(to):
        return copy(
            lt.at[rows(zl, 8)], lt.at[rows(zl, 8)], lt_s.at[to], lt_r.at[zl], at_z(zh * NT + to)
        )

    for k in range(1, NT):
        lt_copy(lax.rem(zl + k, NT)).start()

    def zs_copy(q):
        to = 2 * q + c
        return copy(zs.at[rows(q)], zr.at[rows(z)], zs_s.at[q], zr_r.at[z], at_z(to))

    zr_r = zs_r
    for k in range(NZ // 2):
        q = k
        gx_copy(q, c).wait_recv()
        to = 2 * q + c
        s = gi[rows(to), :] + gix[rows(q), :]
        zs[rows(q), :] = s.astype(BF16)

        @pl.when(to != z)
        def _():
            zs_copy(q).start()

        @pl.when(to == z)
        def _():
            gsum[0] = s

    def yr_copy(yi):
        to = 4 * c + yi
        return copy(ys.at[rows(yi)], yr.at[rows(y)], yr_s.at[yi], yr_r.at[y], at_y(to))

    for yi in range(4):
        s = gt[rows(yi * NX + x), :]
        for kx in range(1, NX):
            xx = lax.rem(x + kx, NX)
            slot = rows(yi * NX + xx)
            copy(gtb.at[slot], xr.at[slot], xr_s.at[0, 0], xr_r.at[yi, xx], other).wait_recv()
            s = s + xr[slot, :].astype(F32)
        ys[rows(yi), :] = s.astype(BF16)

        @pl.when(4 * c + yi != y)
        def _():
            yr_copy(yi).start()

        @pl.when(4 * c + yi == y)
        def _():
            gsum[1] = s

    def gl_copy(m):
        return copy(gsum.at[m], gland, gl_s, gl_r, other)

    @pl.when(lax.rem(z, 2) == c)
    def _():
        s = gsum[0]
        for k in range(1, NZ):
            src = lax.rem(z + k, NZ)
            copy(zs.at[rows(0)], zr.at[rows(src)], zs_s.at[0], zr_r.at[src], other).wait_recv()
            s = s + zr[rows(src), :].astype(F32)
        gsum[0] = s

        @pl.when(c == 1)
        def _():
            gl_copy(0).start()

    @pl.when(half == c)
    def _():
        s = gsum[1]
        for k in range(1, NY):
            src = lax.rem(y + k, NY)
            copy(ys.at[rows(0)], yr.at[rows(src)], yr_s.at[0], yr_r.at[src], other).wait_recv()
            s = s + yr[rows(src), :].astype(F32)
        gsum[1] = s

        @pl.when(c == 0)
        def _():
            gl_copy(1).start()

    @pl.when(jnp.logical_and(c == 0, lax.rem(z, 2) == 1))
    def _():
        gl_copy(0).wait_recv()
        gsum[0] = gland[...]

    @pl.when(jnp.logical_and(c == 1, half == 0))
    def _():
        gl_copy(0).wait_recv()
        gsum[1] = gland[...]

    grad = gsum[c]
    un = unit[...]
    dl = inv[:, 0:1] * (grad - un * jnp.sum(un * grad, axis=-1, keepdims=True))
    delta[rows(zl), :] = dl.astype(BF16)

    def d_copy(src, p, right):
        blk = piece(src, p)
        i = src * NP + p
        dev = at_z(lax.rem(z + (1 if right else NZ - 1), NZ))
        return copy(delta.at[blk], delta.at[blk], d_s.at[0 if right else 1, i], d_r.at[i], dev)

    def d_step(src, p, right):
        @pl.when(zl != (NT - 1 if right else 0))
        def _():
            d_copy(src, p, right).start()

    def d_wait(src, p):
        d_copy(src, p, True).wait_recv()

    for p in range(NP):
        d_step(zl, p, True)
        d_step(zl, p, False)
    for k in range(1, NT):
        for p in range(NP):

            @pl.when(zl >= k)
            def _():
                d_wait(zl - k, p)
                d_step(zl - k, p, True)

            @pl.when(zl + k < NT)
            def _():
                d_wait(zl + k, p)
                d_step(zl + k, p, False)

    for k in range(1, NT):
        src = lax.rem(zl + k, NT)
        copy(lt.at[rows(0, 8)], lt.at[rows(src, 8)], lt_s.at[0], lt_r.at[src], other).wait_recv()
    ls = lt[0:8, :]
    for t in range(1, NT):
        ls = ls + lt[8 * t : 8 * t + 8, :]
    lx[rows(x, 8), :] = ls

    g[...] = lax.dot_general(
        fa[...], delta[...], (((0,), (0,)), ((), ())), preferred_element_type=F32
    )

    gb[...] = g[...].astype(BF16)

    def ax_copy(k):
        xx, dev = at_x(k)
        return copy(gb.at[rows(xx)], ax.at[rows(x)], ax_s.at[xx], ax_r.at[x], dev)

    def lx_copy(k):
        xx, dev = at_x(k)
        return copy(lx.at[rows(x, 8)], lx.at[rows(x, 8)], lx_s.at[xx], lx_r.at[x], dev)

    for k in (2, 1, 3):
        ax_copy(k).start()
        lx_copy(k).start()
    s = g[rows(x), :]
    for k in range(1, NX):
        xx = lax.rem(x + k, NX)
        copy(gb.at[rows(0)], ax.at[rows(xx)], ax_s.at[0], ax_r.at[xx], other).wait_recv()
        s = s + ax[rows(xx), :].astype(F32)
        copy(lx.at[rows(0, 8)], lx.at[rows(xx, 8)], lx_s.at[0], lx_r.at[xx], other).wait_recv()
    for k in range(NY):
        ap[k, 0:U, :] = s[:, 128 * k : 128 * (k + 1)]
    for k in range(6):
        ap[k, U : U + 8, :] = s[8 * k : 8 * k + 8, 1024:1152]
    ls = lx[0:8, :]
    for t in range(1, NX):
        ls = ls + lx[8 * t : 8 * t + 8, :]
    ap[6, U : U + 8, :] = ls
    ap[7, U : U + 8, :] = ls

    def ay_copy(to):
        return copy(ap.at[to], ay.at[y], ay_s.at[to], ay_r.at[y], at_y(to))

    for k in (4, 3, 5, 2, 6, 1, 7):
        ay_copy(lax.rem(y + k, NY)).start()
    s = ap[y]
    for k in range(1, NY):
        src = lax.rem(y + k, NY)
        copy(ap.at[0], ay.at[src], ay_s.at[0], ay_r.at[src], other).wait_recv()
        s = s + ay[src]
    a[...] = s
    az_copy = copy(a, az, az_s, az_r, at_z(lax.rem(z + NT, NZ)))
    az_copy.start()
    az_copy.wait()
    ag[y] = s + az[...]

    def ag_copy(to):
        return copy(ag.at[y], ag.at[y], ag_s.at[to], ag_r.at[y], at_y(to))

    for k in (4, 3, 5, 2, 6, 1, 7):
        ag_copy(lax.rem(y + k, NY)).start()
    for k in range(1, NY):
        src = lax.rem(y + k, NY)
        copy(ag.at[0], ag.at[src], ag_s.at[0], ag_r.at[src], other).wait_recv()
    last = jnp.concatenate([ag[k, U : U + 8, :] for k in range(6)], axis=0)
    ob[c, rows(x), :] = jnp.concatenate(
        [ag[k, 0:U, :] for k in range(NY)] + [last], axis=1
    ).astype(BF16)

    def o_copy(k):
        xx, dev = at_x(k)
        blk = ob.at[c, rows(x)]
        return copy(blk, blk, o_s.at[xx], o_r.at[x], dev)

    def oc_copy(xx, m):
        blk = ob.at[m, rows(xx)]
        return copy(blk, blk, oc_s.at[xx], oc_r.at[xx], other)

    for k in (2, 1, 3):
        o_copy(k).start()
    oc_copy(x, c).start()
    for k in range(1, NX):
        xx = lax.rem(x + k, NX)
        blk = ob.at[c, rows(xx)]
        copy(blk, blk, o_s.at[0], o_r.at[xx], other).wait_recv()
        oc_copy(xx, c).start()
    loss_out[0] = jnp.sum(ag[6, U : U + 8, :]) * (1.0 / (NX * NY * NZ * U))
    for xx in range(NX):
        oc_copy(xx, 1 - c).wait_recv()

    for k in range(1, NT):
        to = lax.rem(zl + k, NT)
        part_copy(to).wait_send()
        lt_copy(to).wait_send()
    for d in range(NT):
        for p in range(NP):

            @pl.when(jnp.logical_and(d <= zl, zl != NT - 1))
            def _():
                d_copy(d, p, True).wait_send()

            @pl.when(jnp.logical_and(d >= zl, zl != 0))
            def _():
                d_copy(d, p, False).wait_send()

    @pl.when(c == 0)
    def _():
        img_up(z).wait_send()
        img_down(z).wait_send()
        for s in range(1, 6):
            img_up(lax.rem(z + NZ - s, NZ)).wait_send()
            if s < 5:
                img_down(lax.rem(z + s, NZ)).wait_send()
        for s in range(NZ):
            img_over(s).wait_send()

    @pl.when(jnp.logical_and(c == 1, half == 0))
    def _():
        txt_over().wait_send()

    @pl.when(half == c)
    def _():
        for k in range(1, NY):
            txt_y(lax.rem(y + k, NY)).wait_send()

    for yi in range(4):
        for k in range(1, NX):
            txt_x(yi, k).wait_send()
            xr_copy(yi, k).wait_send()

        @pl.when(4 * c + yi != y)
        def _():
            yr_copy(yi).wait_send()

    lc_copy().wait_send()
    for q in range(NZ // 2):
        gx_copy(q, 1 - c).wait_send()

        @pl.when(2 * q + c != z)
        def _():
            zs_copy(q).wait_send()

    @pl.when(jnp.logical_and(c == 1, lax.rem(z, 2) == 1))
    def _():
        gl_copy(0).wait_send()

    @pl.when(jnp.logical_and(c == 0, half == 0))
    def _():
        gl_copy(1).wait_send()

    for k in range(1, NX):
        ax_copy(k).wait_send()
        lx_copy(k).wait_send()
        o_copy(k).wait_send()
    for k in range(1, NY):
        to = lax.rem(y + k, NY)
        ay_copy(to).wait_send()
        ag_copy(to).wait_send()
    for xx in range(NX):
        oc_copy(xx, c).wait_send()


def on_device(
    image_features, text_features, image_head, text_head, caption_ids, logit_scale, logit_bias
):
    x, y, zh, zl, c = place()
    table = caption_ids.reshape(NY, NX, 2, 2, NT, 24)
    ids_i = lax.dynamic_slice(table, (y, x, 0, 0, 0, 0), (1, 1, 2, 2, NT, 24))
    ids_i = ids_i.reshape(2, 2, NT, 24).transpose(0, 2, 1, 3).reshape(NI, 1)
    ids_t = lax.dynamic_slice(table, (4 * c, 0, zh, 0, zl, 0), (4, NX, 1, 2, 1, 24)).reshape(1, NJ)
    vm = pl.BlockSpec(memory_space=pltpu.VMEM)
    sm = pl.BlockSpec(memory_space=pltpu.SMEM)
    dma = pltpu.SemaphoreType.DMA
    scratch = dict(
        h=((192, E), BF16), fx=((144, 192), BF16), fa=((NT * U, 192), BF16),
        part=((NT * U, E), F32), spart=((NT * U, E), BF16), rpart=((NT * U, E), BF16),
        unit=((U, E), F32), inv=((U, 128), F32),
        img=((NI, E), BF16), txt=((NJ, E), BF16), own=((U, E), BF16),
        ip=((NI, NJ), F32), coef=((NI, NJ), BF16), gi=((NI, E), F32), gt=((NJ, E), F32),
        gix=((NI // 2, E), F32), zs=((NI // 2, E), BF16), zr=((NI, E), BF16),
        gtb=((NJ, E), BF16), xr=((NJ, E), BF16), ys=((4 * U, E), BF16), yr=((NY * U, E), BF16),
        gsum=((2, U, E), F32), gland=((U, E), F32),
        delta=((NT * U, E), BF16), g=((192, E), F32), gb=((192, E), BF16), ax=((192, E), BF16),
        a=((U + 8, 128), F32), ap=((NY, U + 8, 128), F32), ay=((NY, U + 8, 128), F32),
        az=((U + 8, 128), F32), ag=((NY, U + 8, 128), F32),
        lp=((8, 128), F32), lc=((8, 128), F32), lt=((8 * NT, 128), F32), lx=((8 * NX, 128), F32),
    )
    sems = [
        (), (), (), (NT,), (NT,), (2, NZ), (NZ,), (NZ,), (NZ,), (), (), (NY,), (4,), (4, NX), (4, NX),
        (6,), (6,), (6,), (NZ,), (4, NX), (4, NX), (4,), (NY,), (), (), (2, NT * NP), (NT * NP,),
        (NX,), (NX,), (NY,), (NY,), (), (), (NY,), (NY,), (NX,), (NX,), (NX,), (NX,),
        (), (), (NT,), (NT,), (NX,), (NX,),
    ]
    heads, loss = pl.pallas_call(
        kernel,
        out_shape=(
            jax.ShapeDtypeStruct((2, 192, E), BF16),
            jax.ShapeDtypeStruct((1,), F32),
        ),
        in_specs=[
            vm, vm, pl.BlockSpec(memory_space=pl.ANY), pl.BlockSpec(memory_space=pl.ANY),
            vm, vm, sm, sm,
        ],
        out_specs=(vm, sm),
        scratch_shapes=[pltpu.VMEM(*scratch[n]) for n in scratch]
        + [dma(s) if s else dma for s in sems],
        compiler_params=pltpu.CompilerParams(
            collective_id=0, has_side_effects=True, vmem_limit_bytes=56 * 2**20
        ),
        cost_estimate=pl.CostEstimate(
            flops=4 * 10**9, bytes_accessed=10**7, transcendentals=10**6
        ),
        name="siglip",
    )(
        image_features, text_features, image_head, text_head, ids_i, ids_t, logit_scale, logit_bias
    )
    return loss, heads[0].astype(F32), heads[1].astype(F32)


def solution(mesh):
    placed = (
        P("batch", "tower"),
        P("batch", "tower"),
        P("tower", None),
        P("tower", None),
        P(),
        P(),
        P(),
    )
    return jax.shard_map(
        on_device,
        mesh=mesh,
        in_specs=placed,
        out_specs=(P(), P("tower", None), P("tower", None)),
        check_vma=False,
    )
```

```python
import functools

import jax
import jax.numpy as jnp
from jax import lax
from jax.experimental import pallas as pl
from jax.experimental.pallas import tpu as pltpu
from jax.sharding import PartitionSpec as P

MESH = pl.DeviceIdType.MESH
F32, BF16 = jnp.float32, jnp.bfloat16
NX, NY, NZ, NT = 4, 8, 12, 6
E = 1152
U = 48
NP = 3
NI, NJ = NZ * U, 4 * NX * U
norm_eps = 1e-06


def place():
    b = lax.axis_index("batch")
    zl = lax.axis_index("tower")
    c = lax.rem(b, 2)
    zh = lax.rem(b // 2, 2)
    x = lax.rem(b // 4, NX)
    y = b // 16
    return x, y, zh, zl, c


def device(x, y, z, c):
    return (((y * NX + x) * 2 + z // NT) * 2 + c, lax.rem(z, NT))


def rows(i, n=U):
    return pl.ds(pl.multiple_of(i * n, 8 if n % 16 else 16), n)


def copy(src, dst, ss, rs, dev):
    return pltpu.make_async_remote_copy(
        src_ref=src, dst_ref=dst, send_sem=ss, recv_sem=rs, device_id=dev, device_id_type=MESH
    )


def kernel(
    fi, ft, hi, ht, ids_i, ids_t, scale, bias,
    ob, loss_out,
    h, fx, fa, part, spart, rpart, unit, inv,
    img, txt, own, ip, coef, gi, gt, gix, zs, zr, gtb, xr, ys, yr, gsum, gland,
    delta, g, gb, ax, a, ap, ay, az, ag, lp, lc, lt, lx,
    hsem, fs, fr, ps, pr, isn, irc, ic_s, ic_r, ts_s, ts_r, ys_s, ys_r, xs_s, xs_r,
    gx_s, gx_r, zs_s, zs_r, xr_s, xr_r, yr_s, yr_r, gl_s, gl_r, d_s, d_r,
    ax_s, ax_r, ay_s, ay_r, az_s, az_r, ag_s, ag_r, o_s, o_r, oc_s, oc_r,
    lc_s, lc_r, lt_s, lt_r, lx_s, lx_r,
):
    x, y, zh, zl, c = place()
    z = zh * NT + zl
    other = device(x, y, z, 1 - c)
    half = y // 4

    def at_x(k):
        xx = lax.rem(x + k, NX)
        return xx, device(xx, y, z, c)

    def at_y(yy):
        return device(x, yy, z, c)

    def at_z(zz):
        return device(x, y, zz, c)

    @pl.when(c == 0)
    def _():
        pltpu.make_async_copy(hi, h, hsem).start()

    @pl.when(c == 1)
    def _():
        pltpu.make_async_copy(ht, h, hsem).start()

    barrier = pltpu.get_barrier_semaphore()

    def greet(dev):
        pl.semaphore_signal(barrier, inc=1, device_id=dev, device_id_type=MESH)

    greet(other)
    for k in range(1, NX):
        greet(at_x(k)[1])
    for k in range(1, NY):
        greet(at_y(lax.rem(y + k, NY)))
    for k in range(1, NZ):
        greet(at_z(lax.rem(z + k, NZ)))
    pl.semaphore_wait(barrier, 1 + NX - 1 + NY - 1 + NZ - 1)

    @pl.when(c == 0)
    def _():
        copy(ft, fx, fs, fr, other).start()

    @pl.when(c == 1)
    def _():
        copy(fi, fx, fs, fr, other).start()

    copy(ft, fx, fs, fr, other).wait()

    def gather_features(first, second):
        fst = first[...].astype(F32)
        snd = second[...].astype(F32)
        for t in range(NT):
            fa[t * U : (t + 1) * U, :] = jnp.concatenate(
                [fst[24 * t : 24 * t + 24], snd[24 * t : 24 * t + 24]], axis=0
            ).astype(BF16)

    @pl.when(c == 0)
    def _():
        gather_features(fi, fx)

    @pl.when(c == 1)
    def _():
        gather_features(fx, ft)

    pltpu.make_async_copy(hi, h, hsem).wait()

    def piece(d, p):
        return rows(d * NP + p, U // NP)

    part[...] = jnp.dot(fa[...], h[...], preferred_element_type=F32)
    spart[...] = part[...].astype(BF16)

    def part_copy(to):
        return copy(
            spart.at[rows(to)], rpart.at[rows(zl)], ps.at[to], pr.at[zl], at_z(zh * NT + to)
        )

    def part_wait(src):
        copy(spart.at[rows(0)], rpart.at[rows(src)], ps.at[0], pr.at[src], other).wait_recv()

    for k in range(1, NT):
        part_copy(lax.rem(zl + k, NT)).start()
    raw = part[rows(zl), :]
    for k in range(1, NT):
        src = lax.rem(zl + k, NT)
        part_wait(src)
        raw = raw + rpart[rows(src), :].astype(F32)
    inverse = lax.rsqrt(jnp.sum(raw * raw, axis=-1, keepdims=True) + norm_eps)
    raw = raw * inverse
    unit[...] = raw
    inv[...] = jnp.broadcast_to(inverse, (U, 128))
    own[...] = raw.astype(BF16)

    mine = rows(lax.rem(y, 4) * NX + x)

    def img_up(slot):
        return copy(
            img.at[rows(slot)], img.at[rows(slot)], isn.at[0, slot], irc.at[slot],
            at_z(lax.rem(z + 1, NZ)),
        )

    def img_down(slot):
        return copy(
            img.at[rows(slot)], img.at[rows(slot)], isn.at[1, slot], irc.at[slot],
            at_z(lax.rem(z + NZ - 1, NZ)),
        )

    def img_over(slot):
        return copy(
            img.at[rows(slot)], img.at[rows(slot)], ic_s.at[slot], ic_r.at[slot], other
        )

    def txt_over():
        return copy(own, txt.at[mine], ts_s, ts_r, other)

    def txt_y(to):
        return copy(txt.at[mine], txt.at[mine], ys_s.at[to], ys_r.at[lax.rem(y, 4)], at_y(to))

    def txt_x(yi, k):
        xx, dev = at_x(k)
        slot = rows(yi * NX + x)
        return copy(txt.at[slot], txt.at[slot], xs_s.at[yi, xx], xs_r.at[yi, x], dev)

    def txt_y_send():
        for k in (4, 3, 5, 2, 6, 1, 7):
            txt_y(lax.rem(y + k, NY)).start()

    def txt_forward(k):
        yi = lax.rem(y + k, 4)

        @pl.when(4 * c + yi != y)
        def _():
            slot = rows(yi * NX + x)
            copy(txt.at[slot], txt.at[slot], ys_s.at[0], ys_r.at[yi], other).wait_recv()

        for kx in (2, 1, 3):
            txt_x(yi, kx).start()

    @pl.when(c == 1)
    def _():
        @pl.when(half == 0)
        def _():
            txt_over().start()

        @pl.when(half == 1)
        def _():
            txt[mine, :] = own[...]
            txt_y_send()

        for k in range(4):
            txt_forward(k)
        for s in range(NZ):
            img_over(s).wait_recv()

    @pl.when(c == 0)
    def _():
        img[rows(z), :] = own[...]
        img_up(z).start()
        img_down(z).start()
        img_over(z).start()

        @pl.when(half == 0)
        def _():
            txt_over().wait_recv()
            txt_y_send()

        for s in range(1, 7):
            lo = lax.rem(z + NZ - s, NZ)
            hi_ = lax.rem(z + s, NZ)
            img_up(lo).wait_recv()
            if s < 6:
                img_up(lo).start()
            img_over(lo).start()
            if s < 6:
                img_down(hi_).wait_recv()
                if s < 5:
                    img_down(hi_).start()
                img_over(hi_).start()
            if s <= 4:
                txt_forward(s - 1)

    for yi in range(4):
        for k in range(1, NX):
            xx = lax.rem(x + k, NX)
            slot = rows(yi * NX + xx)
            copy(txt.at[slot], txt.at[slot], xs_s.at[0, 0], xs_r.at[yi, xx], other).wait_recv()

    ip[...] = lax.dot_general(
        img[...], txt[...], (((1,), (1,)), ((), ())), preferred_element_type=F32
    )
    mult, shift = scale[0], bias[0]
    factor = mult * (1.0 / (NX * NY * NZ * U))

    def pairs(i, total):
        r = rows(i)
        logits = mult * ip[r, :] + shift
        same = ids_i[r, :] == ids_t[...]
        v = jnp.where(same, logits, -logits)
        e = jnp.exp(-jnp.abs(v))
        d = 1.0 / (1.0 + e)
        sig = jnp.where(v >= 0, e * d, d)
        coef[r, :] = (jnp.where(same, -factor, factor) * sig).astype(BF16)
        ls = jnp.log1p(e) - jnp.minimum(v, 0.0)
        ls = jnp.sum(ls.reshape(U // 8, 8, NJ), axis=0)
        for j in range(NJ // 128):
            total = total + ls[:, 128 * j : 128 * (j + 1)]
        return total

    lp[...] = lax.fori_loop(0, NZ, pairs, jnp.zeros((8, 128), F32))

    def lc_copy():
        return copy(lp, lc, lc_s, lc_r, other)

    lc_copy().start()

    def gx_copy(q, to_core):
        return copy(gi.at[rows(2 * q + to_core)], gix.at[rows(q)], gx_s.at[q], gx_r.at[q], other)

    def xr_copy(yi, k):
        xx, dev = at_x(k)
        return copy(
            gtb.at[rows(yi * NX + xx)], xr.at[rows(yi * NX + x)], xr_s.at[yi, xx], xr_r.at[yi, x],
            dev,
        )

    for ib in range(3):
        blk = slice(ib * NI // 3, (ib + 1) * NI // 3)
        gi[blk, :] = jnp.dot(coef[blk, :], txt[...], preferred_element_type=F32)
        for q in (2 * ib, 2 * ib + 1):
            gx_copy(q, 1 - c).start()

    for jb in range(2):
        blk = slice(jb * NJ // 2, (jb + 1) * NJ // 2)
        gt[blk, :] = lax.dot_general(
            coef[:, blk], img[...], (((0,), (0,)), ((), ())), preferred_element_type=F32
        )
        gtb[blk, :] = gt[blk, :].astype(BF16)
        for yi in (2 * jb, 2 * jb + 1):
            for kx in (2, 1, 3):
                xr_copy(yi, kx).start()

    lc_copy().wait_recv()
    lt[rows(zl, 8), :] = lp[...] + lc[...]

    def lt_copy(to):
        return copy(
            lt.at[rows(zl, 8)], lt.at[rows(zl, 8)], lt_s.at[to], lt_r.at[zl], at_z(zh * NT + to)
        )

    for k in range(1, NT):
        lt_copy(lax.rem(zl + k, NT)).start()

    def zs_copy(q):
        to = 2 * q + c
        return copy(zs.at[rows(q)], zr.at[rows(z)], zs_s.at[q], zr_r.at[z], at_z(to))

    zr_r = zs_r
    for k in range(NZ // 2):
        q = k
        gx_copy(q, c).wait_recv()
        to = 2 * q + c
        s = gi[rows(to), :] + gix[rows(q), :]
        zs[rows(q), :] = s.astype(BF16)

        @pl.when(to != z)
        def _():
            zs_copy(q).start()

        @pl.when(to == z)
        def _():
            gsum[0] = s

    def yr_copy(yi):
        to = 4 * c + yi
        return copy(ys.at[rows(yi)], yr.at[rows(y)], yr_s.at[yi], yr_r.at[y], at_y(to))

    for yi in range(4):
        s = gt[rows(yi * NX + x), :]
        for kx in range(1, NX):
            xx = lax.rem(x + kx, NX)
            slot = rows(yi * NX + xx)
            copy(gtb.at[slot], xr.at[slot], xr_s.at[0, 0], xr_r.at[yi, xx], other).wait_recv()
            s = s + xr[slot, :].astype(F32)
        ys[rows(yi), :] = s.astype(BF16)

        @pl.when(4 * c + yi != y)
        def _():
            yr_copy(yi).start()

        @pl.when(4 * c + yi == y)
        def _():
            gsum[1] = s

    def gl_copy(m):
        return copy(gsum.at[m], gland, gl_s, gl_r, other)

    @pl.when(lax.rem(z, 2) == c)
    def _():
        s = gsum[0]
        for k in range(1, NZ):
            src = lax.rem(z + k, NZ)
            copy(zs.at[rows(0)], zr.at[rows(src)], zs_s.at[0], zr_r.at[src], other).wait_recv()
            s = s + zr[rows(src), :].astype(F32)
        gsum[0] = s

        @pl.when(c == 1)
        def _():
            gl_copy(0).start()

    @pl.when(half == c)
    def _():
        s = gsum[1]
        for k in range(1, NY):
            src = lax.rem(y + k, NY)
            copy(ys.at[rows(0)], yr.at[rows(src)], yr_s.at[0], yr_r.at[src], other).wait_recv()
            s = s + yr[rows(src), :].astype(F32)
        gsum[1] = s

        @pl.when(c == 0)
        def _():
            gl_copy(1).start()

    @pl.when(jnp.logical_and(c == 0, lax.rem(z, 2) == 1))
    def _():
        gl_copy(0).wait_recv()
        gsum[0] = gland[...]

    @pl.when(jnp.logical_and(c == 1, half == 0))
    def _():
        gl_copy(0).wait_recv()
        gsum[1] = gland[...]

    grad = gsum[c]
    un = unit[...]
    dl = inv[:, 0:1] * (grad - un * jnp.sum(un * grad, axis=-1, keepdims=True))
    delta[rows(zl), :] = dl.astype(BF16)

    def d_copy(src, p, right):
        blk = piece(src, p)
        i = src * NP + p
        dev = at_z(lax.rem(z + (1 if right else NZ - 1), NZ))
        return copy(delta.at[blk], delta.at[blk], d_s.at[0 if right else 1, i], d_r.at[i], dev)

    def d_step(src, p, right):
        @pl.when(zl != (NT - 1 if right else 0))
        def _():
            d_copy(src, p, right).start()

    def d_wait(src, p):
        d_copy(src, p, True).wait_recv()

    for p in range(NP):
        d_step(zl, p, True)
        d_step(zl, p, False)
    for k in range(1, NT):
        for p in range(NP):

            @pl.when(zl >= k)
            def _():
                d_wait(zl - k, p)
                d_step(zl - k, p, True)

            @pl.when(zl + k < NT)
            def _():
                d_wait(zl + k, p)
                d_step(zl + k, p, False)

    for k in range(1, NT):
        src = lax.rem(zl + k, NT)
        copy(lt.at[rows(0, 8)], lt.at[rows(src, 8)], lt_s.at[0], lt_r.at[src], other).wait_recv()
    ls = lt[0:8, :]
    for t in range(1, NT):
        ls = ls + lt[8 * t : 8 * t + 8, :]
    lx[rows(x, 8), :] = ls

    g[...] = lax.dot_general(
        fa[...], delta[...], (((0,), (0,)), ((), ())), preferred_element_type=F32
    )

    gb[...] = g[...].astype(BF16)

    def ax_copy(k):
        xx, dev = at_x(k)
        return copy(gb.at[rows(xx)], ax.at[rows(x)], ax_s.at[xx], ax_r.at[x], dev)

    def lx_copy(k):
        xx, dev = at_x(k)
        return copy(lx.at[rows(x, 8)], lx.at[rows(x, 8)], lx_s.at[xx], lx_r.at[x], dev)

    for k in (2, 1, 3):
        ax_copy(k).start()
        lx_copy(k).start()
    s = g[rows(x), :]
    for k in range(1, NX):
        xx = lax.rem(x + k, NX)
        copy(gb.at[rows(0)], ax.at[rows(xx)], ax_s.at[0], ax_r.at[xx], other).wait_recv()
        s = s + ax[rows(xx), :].astype(F32)
        copy(lx.at[rows(0, 8)], lx.at[rows(xx, 8)], lx_s.at[0], lx_r.at[xx], other).wait_recv()
    for k in range(NY):
        ap[k, 0:U, :] = s[:, 128 * k : 128 * (k + 1)]
    for k in range(6):
        ap[k, U : U + 8, :] = s[8 * k : 8 * k + 8, 1024:1152]
    ls = lx[0:8, :]
    for t in range(1, NX):
        ls = ls + lx[8 * t : 8 * t + 8, :]
    ap[6, U : U + 8, :] = ls
    ap[7, U : U + 8, :] = ls

    def ay_copy(to):
        return copy(ap.at[to], ay.at[y], ay_s.at[to], ay_r.at[y], at_y(to))

    for k in (4, 3, 5, 2, 6, 1, 7):
        ay_copy(lax.rem(y + k, NY)).start()
    s = ap[y]
    for k in range(1, NY):
        src = lax.rem(y + k, NY)
        copy(ap.at[0], ay.at[src], ay_s.at[0], ay_r.at[src], other).wait_recv()
        s = s + ay[src]
    a[...] = s
    az_copy = copy(a, az, az_s, az_r, at_z(lax.rem(z + NT, NZ)))
    az_copy.start()
    az_copy.wait()
    ag[y] = s + az[...]

    def ag_copy(to):
        return copy(ag.at[y], ag.at[y], ag_s.at[to], ag_r.at[y], at_y(to))

    for k in (4, 3, 5, 2, 6, 1, 7):
        ag_copy(lax.rem(y + k, NY)).start()
    for k in range(1, NY):
        src = lax.rem(y + k, NY)
        copy(ag.at[0], ag.at[src], ag_s.at[0], ag_r.at[src], other).wait_recv()
    last = jnp.concatenate([ag[k, U : U + 8, :] for k in range(6)], axis=0)
    ob[c, rows(x), :] = jnp.concatenate(
        [ag[k, 0:U, :] for k in range(NY)] + [last], axis=1
    ).astype(BF16)

    def o_copy(k):
        xx, dev = at_x(k)
        blk = ob.at[c, rows(x)]
        return copy(blk, blk, o_s.at[xx], o_r.at[x], dev)

    def oc_copy(xx, m):
        blk = ob.at[m, rows(xx)]
        return copy(blk, blk, oc_s.at[xx], oc_r.at[xx], other)

    for k in (2, 1, 3):
        o_copy(k).start()
    oc_copy(x, c).start()
    for k in range(1, NX):
        xx = lax.rem(x + k, NX)
        blk = ob.at[c, rows(xx)]
        copy(blk, blk, o_s.at[0], o_r.at[xx], other).wait_recv()
        oc_copy(xx, c).start()
    loss_out[0] = jnp.sum(ag[6, U : U + 8, :]) * (1.0 / (NX * NY * NZ * U))
    for xx in range(NX):
        oc_copy(xx, 1 - c).wait_recv()

    for k in range(1, NT):
        to = lax.rem(zl + k, NT)
        part_copy(to).wait_send()
        lt_copy(to).wait_send()
    for d in range(NT):
        for p in range(NP):

            @pl.when(jnp.logical_and(d <= zl, zl != NT - 1))
            def _():
                d_copy(d, p, True).wait_send()

            @pl.when(jnp.logical_and(d >= zl, zl != 0))
            def _():
                d_copy(d, p, False).wait_send()

    @pl.when(c == 0)
    def _():
        img_up(z).wait_send()
        img_down(z).wait_send()
        for s in range(1, 6):
            img_up(lax.rem(z + NZ - s, NZ)).wait_send()
            if s < 5:
                img_down(lax.rem(z + s, NZ)).wait_send()
        for s in range(NZ):
            img_over(s).wait_send()

    @pl.when(jnp.logical_and(c == 1, half == 0))
    def _():
        txt_over().wait_send()

    @pl.when(half == c)
    def _():
        for k in range(1, NY):
            txt_y(lax.rem(y + k, NY)).wait_send()

    for yi in range(4):
        for k in range(1, NX):
            txt_x(yi, k).wait_send()
            xr_copy(yi, k).wait_send()

        @pl.when(4 * c + yi != y)
        def _():
            yr_copy(yi).wait_send()

    lc_copy().wait_send()
    for q in range(NZ // 2):
        gx_copy(q, 1 - c).wait_send()

        @pl.when(2 * q + c != z)
        def _():
            zs_copy(q).wait_send()

    @pl.when(jnp.logical_and(c == 1, lax.rem(z, 2) == 1))
    def _():
        gl_copy(0).wait_send()

    @pl.when(jnp.logical_and(c == 0, half == 0))
    def _():
        gl_copy(1).wait_send()

    for k in range(1, NX):
        ax_copy(k).wait_send()
        lx_copy(k).wait_send()
        o_copy(k).wait_send()
    for k in range(1, NY):
        to = lax.rem(y + k, NY)
        ay_copy(to).wait_send()
        ag_copy(to).wait_send()
    for xx in range(NX):
        oc_copy(xx, c).wait_send()


def on_device(
    image_features, text_features, image_head, text_head, caption_ids, logit_scale, logit_bias
):
    x, y, zh, zl, c = place()
    table = caption_ids.reshape(NY, NX, 2, 2, NT, 24)
    ids_i = lax.dynamic_slice(table, (y, x, 0, 0, 0, 0), (1, 1, 2, 2, NT, 24))
    ids_i = ids_i.reshape(2, 2, NT, 24).transpose(0, 2, 1, 3).reshape(NI, 1)
    ids_t = lax.dynamic_slice(table, (4 * c, 0, zh, 0, zl, 0), (4, NX, 1, 2, 1, 24)).reshape(1, NJ)
    vm = pl.BlockSpec(memory_space=pltpu.VMEM)
    sm = pl.BlockSpec(memory_space=pltpu.SMEM)
    dma = pltpu.SemaphoreType.DMA
    scratch = dict(
        h=((192, E), BF16), fx=((144, 192), BF16), fa=((NT * U, 192), BF16),
        part=((NT * U, E), F32), spart=((NT * U, E), BF16), rpart=((NT * U, E), BF16),
        unit=((U, E), F32), inv=((U, 128), F32),
        img=((NI, E), BF16), txt=((NJ, E), BF16), own=((U, E), BF16),
        ip=((NI, NJ), F32), coef=((NI, NJ), BF16), gi=((NI, E), F32), gt=((NJ, E), F32),
        gix=((NI // 2, E), F32), zs=((NI // 2, E), BF16), zr=((NI, E), BF16),
        gtb=((NJ, E), BF16), xr=((NJ, E), BF16), ys=((4 * U, E), BF16), yr=((NY * U, E), BF16),
        gsum=((2, U, E), F32), gland=((U, E), F32),
        delta=((NT * U, E), BF16), g=((192, E), F32), gb=((192, E), BF16), ax=((192, E), BF16),
        a=((U + 8, 128), F32), ap=((NY, U + 8, 128), F32), ay=((NY, U + 8, 128), F32),
        az=((U + 8, 128), F32), ag=((NY, U + 8, 128), F32),
        lp=((8, 128), F32), lc=((8, 128), F32), lt=((8 * NT, 128), F32), lx=((8 * NX, 128), F32),
    )
    sems = [
        (), (), (), (NT,), (NT,), (2, NZ), (NZ,), (NZ,), (NZ,), (), (), (NY,), (4,), (4, NX), (4, NX),
        (6,), (6,), (6,), (NZ,), (4, NX), (4, NX), (4,), (NY,), (), (), (2, NT * NP), (NT * NP,),
        (NX,), (NX,), (NY,), (NY,), (), (), (NY,), (NY,), (NX,), (NX,), (NX,), (NX,),
        (), (), (NT,), (NT,), (NX,), (NX,),
    ]
    heads, loss = pl.pallas_call(
        kernel,
        out_shape=(
            jax.ShapeDtypeStruct((2, 192, E), BF16),
            jax.ShapeDtypeStruct((1,), F32),
        ),
        in_specs=[
            vm, vm, pl.BlockSpec(memory_space=pl.ANY), pl.BlockSpec(memory_space=pl.ANY),
            vm, vm, sm, sm,
        ],
        out_specs=(vm, sm),
        scratch_shapes=[pltpu.VMEM(*scratch[n]) for n in scratch]
        + [dma(s) if s else dma for s in sems],
        compiler_params=pltpu.CompilerParams(
            collective_id=0, has_side_effects=True, vmem_limit_bytes=56 * 2**20
        ),
        cost_estimate=pl.CostEstimate(
            flops=4 * 10**9, bytes_accessed=10**7, transcendentals=10**6
        ),
        name="siglip",
    )(
        image_features, text_features, image_head, text_head, ids_i, ids_t, logit_scale, logit_bias
    )
    return loss, heads[0].astype(F32), heads[1].astype(F32)


def solution(mesh):
    placed = (
        P("batch", "tower"),
        P("batch", "tower"),
        P("tower", None),
        P("tower", None),
        P(),
        P(),
        P(),
    )
    return jax.shard_map(
        on_device,
        mesh=mesh,
        in_specs=placed,
        out_specs=(P(), P("tower", None), P("tower", None)),
        check_vma=False,
    )
```
